32 devices in a mesh: wall: 4 (over y, x), stream: 8 (over z, core).
Axes of the slice: x: 2, y: 2, z: 4, core: 2. Of those that a mesh axis runs over, the one named last changes fastest.
Arguments:
- velocity: float32 [3, 32, 128, 128], P(None, 'wall', 'stream'), may hold values from -6 to 6
- sample_block: int32 [4, 32], P('wall', 'stream'), may hold values from 0 to 127
- sample_member: int32 [4, 32, 1], P('wall', 'stream'), may hold values from 0 to 3; in each aligned block of 4 rows (0 to 3, 4 to 7, ..., all dimensions but the last counted through in order) at most 2 rows name the same one
- k_first: bfloat16 [4, 54, 64], P('wall'), may hold values from -6 to 6
- k_second: bfloat16 [4, 27, 64, 64], P('wall'), may hold values from -6 to 6
- w_hidden: bfloat16 [4, 2048, 2048], P('wall'), may hold values from -6 to 6
- w_out: bfloat16 [4, 2048, 2], P('wall'), may hold values from -6 to 6
Outputs:
- new_field: float32 [3, 32, 128, 128], P(None, 'wall', 'stream')
- stress: float32 [2, 4, 32], P(None, 'wall', 'stream')
- new_k_first: float32 [4, 54, 64], P('wall')
- new_k_second: float32 [4, 27, 64, 64], P('wall')
- new_w_hidden: float32 [4, 2048, 2048], P('wall', 'stream')
- new_w_out: float32 [4, 2048, 2], P('wall')
The draws below stay inside these ranges and needn't reach their ends.
Inputs may be any that keep to these rules, and one draw needn't show every extreme that they name: `sample_block`: A block of the slab's own points, numbered as in the reference program. `sample_member`: in the list of one slab at most 2 samples name the same member; in every draw some slab names some member exactly 2 times.
All inputs are finite; a program needn't handle non-finite values.
Results may differ from the reference program's by a relative error of at most 0.0064.
Values may be sent and summed in bfloat16 or wider, within the bound.
A program may use at most 128 MiB of HBM per device.

```python
import math
import jax
import jax.numpy as jnp
import numpy as np
from jax import lax

P_SIZE = 8
EY = 1
EX = 2
PY = 4
PX = 4
PZ = 8
CH = 64
HID = 2048
CAP = 2
SAMPLES = 4
NBLK = 128
FEAT_IN = 256
FEATS = 2048
NY = 32
NX = 128
NZ = 128
MEMBERS = 4
N_WALL = 4
N_STREAM = 8


def place_ends(values, key, smallest, largest):
    spot = [jax.random.randint(jax.random.fold_in(key, axis), (), 0, length) for axis, length in enumerate(values.shape)]
    widest = values.shape.index(max(values.shape))
    beside = spot[:widest] + [(spot[widest] + 1) % values.shape[widest]] + spot[widest + 1:]
    return values.at[tuple(spot)].set(smallest).at[tuple(beside)].set(largest)


def levels(own_key, extent, shards, low, top_value):
    def one(dim, blocks):
        heights = jax.random.uniform(jax.random.fold_in(jax.random.fold_in(own_key, 6), dim), (blocks,), jnp.float32, low / len(shards), top_value / len(shards))
        return jnp.repeat(jnp.exp(heights), extent[dim] // blocks).reshape((-1,) + (1,) * (len(extent) - dim - 1))

    level = one(*shards[0])
    for cut in shards[1:]:
        level = level * one(*cut)
    return level


def shared_out(rng, own, number, rows, count, top, reach, skew):
    order = jax.random.permutation(rng, count)
    packed, usual = shares(count, rows * top, reach, skew, True), shares(count, rows * top, reach, skew, False)
    places = jnp.arange(count)

    def named(lengths, turn):
        used = int((lengths > 0).sum())
        fixed = max(1, used // 4)
        moved = fixed + (places - fixed + turn * (used - fixed)) % max(1, count - fixed)
        return jnp.zeros((count,), jnp.int32).at[order[jnp.where(places < fixed, places, moved)]].set(jnp.asarray(lengths, jnp.int32))

    lengths = jnp.where(number % 4 == 0, named(packed, number // 4), named(usual, number - number // 4 - 1))
    mixed = jax.random.permutation(jax.random.fold_in(own, 3), count)
    source_of, receiver = mixed[0:count // 2 * 2:2], mixed[1:count // 2 * 2:2]
    room = jnp.minimum(lengths[source_of] - 1, reach - lengths[receiver]) // 2
    room = jnp.where((source_of == order[0]) | (receiver == order[0]) | (lengths[receiver] == 0), 0, jnp.maximum(room, 0))
    moved = jax.random.randint(jax.random.fold_in(own, 4), (count // 2,), 0, 1 << 20) % (room + 1)
    lengths = lengths.at[source_of].add(-moved).at[receiver].add(moved)
    items = jnp.searchsorted(jnp.cumsum(lengths), jnp.arange(rows * top), side="right").astype(jnp.int32)
    table = items.reshape(top, rows).T
    table = table[jax.random.permutation(jax.random.fold_in(own, 1), rows)]
    turn = jax.random.randint(jax.random.fold_in(own, 2), (rows, 1), 0, top)
    return jnp.take_along_axis(table, (jnp.arange(top)[None, :] + turn) % top, axis=1)


def shares(number_of, total, bound, skew, full):
    portions = [(1 << 20) // math.isqrt(standing ** skew) + 1 for standing in range(1, number_of + 1)]
    largest = bound if full else min(bound, max(-(-total // number_of), total * portions[0] // sum(portions)))
    least = 1 if total - largest >= number_of - 1 else 0
    counts, spare = [largest] + [least] * (number_of - 1), total - largest - least * (number_of - 1)
    while spare > 0:
        candidates = [i for i in range(1, number_of) if counts[i] < largest] or [i for i in range(1, number_of) if counts[i] < bound]
        mass, remaining = sum([portions[i] for i in candidates]), spare
        for i in candidates:
            extra = min(bound - counts[i], max(1, remaining * portions[i] // mass), spare)
            counts[i] = counts[i] + extra
            spare = spare - extra
    return np.array(counts)


def scatter_about(stream_key, shape, deviation, reach, pieces=(), held_as=jnp.bfloat16):
    drawn = deviation * jax.random.normal(stream_key, shape, jnp.float32)
    if pieces:
        drawn = drawn * levels(stream_key, shape, pieces, -0.22, 0.18)
    return jnp.clip(drawn, -reach, reach).astype(held_as)


def setup_inputs(seed: int = 0) -> dict:
    key_list = jax.random.split(jax.random.key(seed), 8)
    velocity = scatter_about(key_list[0], (3, NY, NX, NZ), 1.0, 6.0, ((1, 4), (2, 8)), jnp.float32)
    sample_block = place_ends(jax.random.randint(key_list[1], (N_WALL, N_STREAM * SAMPLES), 0, NBLK), jax.random.fold_in(key_list[1], 1), 0, NBLK - 1).astype(jnp.int32)
    sample_member_keys = jax.random.split(jax.random.fold_in(key_list[2], 1), N_WALL * (N_STREAM * SAMPLES) // SAMPLES)
    sample_member_turns = jax.random.permutation(jax.random.fold_in(key_list[2], 3), N_WALL * (N_STREAM * SAMPLES) // SAMPLES)
    sample_member = jax.vmap(lambda own, number: shared_out(jax.random.fold_in(key_list[2], 2), own, number, SAMPLES, N_WALL, 1, CAP, 2))(sample_member_keys, sample_member_turns).reshape((N_WALL, N_STREAM * SAMPLES, 1))
    k_first = scatter_about(key_list[3], (MEMBERS, 54, CH), 1.0, 6.0, ((0, 4),))
    k_second = scatter_about(key_list[4], (MEMBERS, 27, CH, CH), 1.0, 6.0, ((0, 4),))
    w_hidden = scatter_about(key_list[5], (MEMBERS, FEATS, HID), 1.0, 6.0, ((0, 4),))
    w_out = scatter_about(key_list[6], (MEMBERS, HID, 2), 1.0, 6.0, ((0, 4),))
    return {"velocity": velocity, "sample_block": sample_block, "sample_member": sample_member, "k_first": k_first, "k_second": k_second, "w_hidden": w_hidden, "w_out": w_out}


highest = lax.Precision.HIGHEST
time_step = 0.005
relax_rate = 20.0
viscosity = 0.3
learn_rate = 0.5
rms_eps = 1e-06
tap_offsets = [(first_off, second_off, third_off) for first_off in (-1, 0, 1) for second_off in (-1, 0, 1) for third_off in (-1, 0, 1)]

def cheb_tables(points):
    order = points - 1
    node_index = np.arange(points)
    nodes = -np.cos(np.pi * node_index / order)
    end_weight = np.where((node_index == 0) | (node_index == order), 2.0, 1.0)
    parity = (-1.0) ** (node_index[:, None] + node_index[None, :])
    offdiag = 1.0 - np.eye(points)
    spread = nodes[:, None] - nodes[None, :] + np.eye(points)
    deriv = end_weight[:, None] / end_weight[None, :] * parity / spread * offdiag
    deriv = deriv - np.eye(points) * deriv.sum(axis=1)[:, None]
    highpass = parity / (order * end_weight[None, :])
    return (deriv, highpass, 0.5 * order * order)

def along_axis(values, axis, periodic):
    deriv, highpass, lift_half = cheb_tables(P_SIZE)
    moved = jnp.moveaxis(values, axis, -1)
    leading = moved.shape[:-1]
    count = moved.shape[-1] // P_SIZE
    blocks = moved.reshape(leading + (count, P_SIZE))
    slope = jnp.einsum('...ep,qp->...eq', blocks, jnp.asarray(deriv, jnp.float32), precision=highest)
    upper = jnp.einsum('...ep,qp->...eq', blocks, jnp.asarray(highpass, jnp.float32), precision=highest)
    first = blocks[..., 0]
    last = blocks[..., P_SIZE - 1]
    if periodic:
        from_left = jnp.roll(last, 1, axis=-1)
        from_right = jnp.roll(first, -1, axis=-1)
    else:
        zeros_edge = jnp.zeros(leading + (1,), jnp.float32)
        from_left = jnp.concatenate([zeros_edge, last[..., :-1]], axis=-1)
        from_right = jnp.concatenate([first[..., 1:], zeros_edge], axis=-1)
    slope = slope.at[..., 0].add(-lift_half * (from_left - first))
    slope = slope.at[..., P_SIZE - 1].add(lift_half * (from_right - last))
    return (jnp.moveaxis(slope.reshape(moved.shape), -1, axis), jnp.moveaxis(upper.reshape(moved.shape), -1, axis))

def slot_matrix(members, member_count):
    member_hot = (members[..., None] == jnp.arange(member_count, dtype=jnp.int32)).astype(jnp.int32)
    before = jnp.cumsum(member_hot, axis=-2) - member_hot
    ranks = lax.optimization_barrier(jnp.sum(before * member_hot, axis=-1))
    slots = members * CAP + ranks
    return (slots[..., None, :] == jnp.arange(member_count * CAP, dtype=jnp.int32)[:, None]).astype(jnp.float32)

def shifted(grid, offset):
    padded = jnp.pad(grid, ((0, 0), (1, 1), (1, 1), (1, 1), (0, 0)))
    size_y, size_x, size_z = (grid.shape[1], grid.shape[2], grid.shape[3])
    return padded[:, 1 + offset[0]:1 + offset[0] + size_y, 1 + offset[1]:1 + offset[1] + size_x, 1 + offset[2]:1 + offset[2] + size_z, :]

def silu_slope(value):
    gate = jax.nn.sigmoid(value)
    return gate * (1.0 + value * (1.0 - gate))

def forward_back(patches, aim_rows, valid, k_first, k_second, w_hidden, w_out):
    batch = patches.shape[0]
    channels = k_second.shape[-1]
    inputs = patches.reshape(batch, 2, PY, PX, PZ).transpose(0, 2, 3, 4, 1)
    columns = jnp.concatenate([shifted(inputs, offset) for offset in tap_offsets], axis=-1).reshape(-1, 54)
    scale_one = 1.0 / math.sqrt(54.0)
    scale_two = 1.0 / math.sqrt(27.0 * channels)
    scale_three = 1.0 / math.sqrt(1.0 * w_hidden.shape[0])
    scale_four = 1.0 / math.sqrt(1.0 * w_hidden.shape[1])
    pre_one = jnp.dot(columns, k_first, preferred_element_type=jnp.float32) * scale_one
    hidden_one = jax.nn.silu(pre_one).astype(jnp.bfloat16).reshape(batch, PY, PX, PZ, channels)
    pre_two = jnp.zeros((batch * PY * PX * PZ, channels), jnp.float32)
    for tap_index in range(27):
        moved = shifted(hidden_one, tap_offsets[tap_index]).reshape(-1, channels)
        pre_two = pre_two + jnp.dot(moved, k_second[tap_index], preferred_element_type=jnp.float32)
    pre_two = pre_two * scale_two
    pooled = jax.nn.silu(pre_two).reshape(batch, PY // 2, 2, PX // 2, 2, PZ, channels).mean(axis=(2, 4))
    features = pooled.reshape(batch, -1).astype(jnp.bfloat16)
    pre_three = jnp.dot(features, w_hidden, preferred_element_type=jnp.float32) * scale_three
    hidden_three = jax.nn.silu(pre_three).astype(jnp.bfloat16)
    pred = jnp.dot(hidden_three, w_out, preferred_element_type=jnp.float32) * scale_four
    error = valid.astype(jnp.float32)[:, None] * (pred - aim_rows.astype(jnp.float32))
    grad_out = jnp.dot(hidden_three.astype(jnp.float32).T, error, precision=highest) * scale_four
    delta_three = (jnp.dot(error, w_out.astype(jnp.float32).T, precision=highest) * scale_four * silu_slope(pre_three)).astype(jnp.bfloat16)
    back_feat = jnp.dot(delta_three, w_hidden.T, preferred_element_type=jnp.float32) * scale_three
    back_grid = back_feat.reshape(batch, PY // 2, 1, PX // 2, 1, PZ, channels)
    spread_back = jnp.broadcast_to(back_grid, (batch, PY // 2, 2, PX // 2, 2, PZ, channels)).reshape(-1, channels) * 0.25
    delta_two = (spread_back * silu_slope(pre_two)).astype(jnp.bfloat16)
    delta_grid = delta_two.reshape(batch, PY, PX, PZ, channels)
    grad_two = []
    back_one = jnp.zeros((batch * PY * PX * PZ, channels), jnp.float32)
    for tap_index in range(27):
        offset = tap_offsets[tap_index]
        moved = shifted(hidden_one, offset).reshape(-1, channels)
        grad_two.append(jnp.dot(moved.T, delta_two, preferred_element_type=jnp.float32) * scale_two)
        mirror = (-offset[0], -offset[1], -offset[2])
        back_one = back_one + jnp.dot(shifted(delta_grid, mirror).reshape(-1, channels), k_second[tap_index].T, preferred_element_type=jnp.float32)
    delta_one = (back_one * scale_two * silu_slope(pre_one)).astype(jnp.bfloat16)
    grad_one = jnp.dot(columns.T, delta_one, preferred_element_type=jnp.float32) * scale_one
    return (pred, grad_one, jnp.stack(grad_two), grad_out, features, delta_three)

def row_update(weight, grad):
    scale = jnp.sqrt(lax.optimization_barrier(jnp.mean(grad * grad, axis=-1, keepdims=True)) + rms_eps)
    return weight.astype(jnp.float32) - learn_rate * grad / scale

def whole_update(weight, grad):
    scale = jnp.sqrt(jnp.mean(grad * grad) + rms_eps)
    return weight.astype(jnp.float32) - learn_rate * grad / scale

def to_members(values):
    rest = values.shape[3:]
    grid = values.reshape((N_WALL, N_STREAM, N_WALL, CAP) + rest)
    grid = jnp.swapaxes(grid, 0, 2)
    return grid.reshape((N_WALL, N_STREAM * N_WALL * CAP) + rest)

def reference(velocity, sample_block, sample_member, k_first, k_second, w_hidden, w_out):
    grad_x, high_x = along_axis(velocity, 2, True)
    grad_y, high_y = along_axis(velocity, 1, False)
    grad_z, high_z = along_axis(velocity, 3, True)
    advect = velocity[0][None] * grad_x + velocity[1][None] * grad_y + velocity[2][None] * grad_z
    new_field = velocity + time_step * (-advect - relax_rate * (high_x + high_y + high_z))
    rows_y, rows_x, rows_z = (EY * P_SIZE // PY, EX * P_SIZE // PX, NZ // PZ)
    tangent = jnp.stack([velocity[0], velocity[2]]).reshape(2, N_WALL, rows_y, PY, N_STREAM, rows_x, PX, rows_z, PZ)
    blocks = tangent.transpose(1, 4, 2, 5, 7, 0, 3, 6, 8).reshape(N_WALL, N_STREAM, NBLK, FEAT_IN)
    slope_wall = jnp.stack([grad_y[0], grad_y[2]]).reshape(2, N_WALL, rows_y, PY, N_STREAM, rows_x, PX, rows_z, PZ)
    stress_true = (viscosity * lax.optimization_barrier(jnp.mean(slope_wall, axis=(3, 6, 8)))).transpose(1, 3, 2, 4, 5, 0).reshape(N_WALL, N_STREAM, NBLK, 2)
    picked = sample_block.reshape(N_WALL, N_STREAM, SAMPLES)
    members = sample_member.reshape(N_WALL, N_STREAM, SAMPLES)
    take_rows = jax.vmap(jax.vmap(lambda lookup_table, row_index: jnp.take(lookup_table, row_index, axis=0)))
    patch_rows = take_rows(blocks, picked).astype(jnp.bfloat16)
    aim_rows = take_rows(stress_true, picked).astype(jnp.bfloat16)
    select = slot_matrix(members, N_WALL)
    send_rows = jnp.einsum('wtls,wtsf->wtlf', select, patch_rows.astype(jnp.float32), precision=highest).astype(jnp.bfloat16)
    send_aims = jnp.einsum('wtls,wtsf->wtlf', select, aim_rows.astype(jnp.float32), precision=highest).astype(jnp.bfloat16)
    send_valid = lax.optimization_barrier(jnp.sum(select, axis=-1)).astype(jnp.bfloat16)
    bundles = (to_members(send_rows), to_members(send_aims), to_members(send_valid), k_first, k_second, w_hidden, w_out)

    def per_member(bundle):
        pred, grad_one, grad_two, grad_out, features, delta_three = forward_back(bundle[0], bundle[1], bundle[2], bundle[3], bundle[4], bundle[5], bundle[6])
        grad_hidden = jnp.dot(features.T, delta_three, preferred_element_type=jnp.float32) * (1.0 / math.sqrt(1.0 * FEATS))
        return (pred, row_update(bundle[3], grad_one), row_update(bundle[4], grad_two), row_update(bundle[5], grad_hidden), whole_update(bundle[6], grad_out))
    preds, new_k_first, new_k_second, new_w_hidden, new_w_out = lax.map(per_member, bundles)
    back = jnp.swapaxes(preds.reshape(N_WALL, N_STREAM, N_WALL, CAP, 2), 0, 2).reshape(N_WALL, N_STREAM, N_WALL * CAP, 2)
    stress = jnp.einsum('wtls,wtlk->kwts', select, back, precision=highest).reshape(2, N_WALL, N_STREAM * SAMPLES)
    return (new_field, stress, new_k_first, new_k_second, new_w_hidden, new_w_out)
```

```python
import math

import jax
import jax.numpy as jnp
import numpy as np
from jax import lax
from jax.experimental import pallas as pl
from jax.experimental.pallas import tpu as pltpu
from jax.sharding import PartitionSpec as P

P_SIZE = 8
PY = 4
PX = 4
PZ = 8
CAP = 2
FEATS = 2048


highest = lax.Precision.HIGHEST
time_step = 0.005
relax_rate = 20.0
viscosity = 0.3
learn_rate = 0.5
rms_eps = 1e-06
tap_offsets = [
    (first_off, second_off, third_off)
    for first_off in (-1, 0, 1)
    for second_off in (-1, 0, 1)
    for third_off in (-1, 0, 1)
]


def with_halo(shard, sides, width):
    for axis, dim in sides:
        size, length = (lax.axis_size(axis), shard.shape[dim])
        up = [(i, (i + 1) % size) for i in range(size)]
        down = [(j, i) for i, j in up]
        last = lax.slice_in_dim(shard, length - width, length, axis=dim)
        first = lax.slice_in_dim(shard, 0, width, axis=dim)
        before = lax.ppermute(last, axis, up)
        after = lax.ppermute(first, axis, down)
        shard = jnp.concatenate([before, shard, after], axis=dim)
    return shard


def cheb_tables(points):
    order = points - 1
    node_index = np.arange(points)
    nodes = -np.cos(np.pi * node_index / order)
    end_weight = np.where((node_index == 0) | (node_index == order), 2.0, 1.0)
    parity = (-1.0) ** (node_index[:, None] + node_index[None, :])
    offdiag = 1.0 - np.eye(points)
    spread = nodes[:, None] - nodes[None, :] + np.eye(points)
    deriv = end_weight[:, None] / end_weight[None, :] * parity / spread * offdiag
    deriv = deriv - np.eye(points) * deriv.sum(axis=1)[:, None]
    highpass = parity / (order * end_weight[None, :])
    return (deriv, highpass, 0.5 * order * order)


def axis_matrices(count, periodic):
    deriv, highpass, lift_half = cheb_tables(P_SIZE)
    length = count * P_SIZE
    slope = np.kron(np.eye(count), deriv)
    upper = np.kron(np.eye(count), highpass)
    faces = count if periodic else count - 1
    for element in range(faces):
        last_node = element * P_SIZE + P_SIZE - 1
        next_node = (element + 1) % count * P_SIZE
        slope[last_node, next_node] += lift_half
        slope[last_node, last_node] -= lift_half
        slope[next_node, last_node] -= lift_half
        slope[next_node, next_node] += lift_half
    if not periodic:
        slope[0, 0] += lift_half
        slope[length - 1, length - 1] -= lift_half
    paired = jnp.asarray(np.concatenate([slope, upper], axis=0), jnp.float32)
    return (paired, lift_half)


def slot_matrix(members, member_count):
    member_hot = (members[..., None] == jnp.arange(member_count, dtype=jnp.int32)).astype(jnp.int32)
    before = jnp.cumsum(member_hot, axis=-2) - member_hot
    ranks = jnp.sum(before * member_hot, axis=-1)
    slots = members * CAP + ranks
    return (slots[..., None, :] == jnp.arange(member_count * CAP, dtype=jnp.int32)[:, None]).astype(
        jnp.float32
    )


def sigmoid(value):
    return 1.0 / (1.0 + jnp.exp(-value))


def silu_slope(value):
    gate = sigmoid(value)
    return gate * (1.0 + value * (1.0 - gate))


def z_shifts(grid, sign):
    edge = jnp.zeros((16, 1, grid.shape[2], grid.shape[-1]), grid.dtype)
    before = jnp.concatenate([edge, grid[:, :-1]], axis=1)
    after = jnp.concatenate([grid[:, 1:], edge], axis=1)
    parts = [before, grid, after] if sign > 0 else [after, grid, before]
    return jnp.concatenate([part.reshape(-1, grid.shape[-1]) for part in parts], axis=-1)


def window(padded, first, second):
    return padded[1 + first : 5 + first, 1 + second : 5 + second].reshape(-1, padded.shape[-1])


def clear_border(padded):
    row = jnp.zeros((1, 6) + padded.shape[2:], padded.dtype)
    column = jnp.zeros((6, 1) + padded.shape[2:], padded.dtype)
    padded[0:1] = row
    padded[5:6] = row
    padded[:, 0:1] = column
    padded[:, 5:6] = column


def matmul(left, right, dims=((1,), (0,))):
    return lax.dot_general(left, right, (dims, ((), ())), preferred_element_type=jnp.float32)


def network(
    rows, aims, valid, k_first, k_second, k_back, w_hbm, w_out,
    pred_ref, grad_one_ref, grad_two_ref, grad_out_ref, feat_ref, delta_ref,
    w_vmem, cols, pre_one, hid_pad, del_pad, mid_pad, pre_two, pooled, w_sem,
):
    batch = rows.shape[0]
    points = 128 * batch
    fetch = pltpu.make_async_copy(w_hbm, w_vmem, w_sem)
    fetch.start()
    scale_one = 1.0 / math.sqrt(54.0)
    scale_two = 1.0 / math.sqrt(1728.0)
    scale_dense = 1.0 / math.sqrt(2048.0)
    clear_border(hid_pad)
    clear_border(del_pad)
    clear_border(mid_pad)
    lane = lax.broadcasted_iota(jnp.int32, (batch, 128), 1)
    at = (lane // 32, (lane // 8) % 4, lane % 8)
    cols[54 * batch : 64 * batch, :] = jnp.zeros((10 * batch, 128), jnp.float32)
    channel = [rows[:, 0:128].astype(jnp.float32), rows[:, 128:256].astype(jnp.float32)]
    for tap, offset in enumerate(tap_offsets):
        inside = None
        for place, step, size in zip(at, offset, (4, 4, 8)):
            if step:
                good = (place + step >= 0) & (place + step < size)
                inside = good if inside is None else inside & good
        turn = (-(offset[0] * 32 + offset[1] * 8 + offset[2])) % 128
        for c in range(2):
            moved = channel[c] if turn == 0 else pltpu.roll(channel[c], turn, 1)
            if inside is not None:
                moved = jnp.where(inside, moved, 0.0)
            cols[(2 * tap + c) * batch : (2 * tap + c + 1) * batch, :] = moved
    columns = jnp.concatenate(
        [cols[pl.ds(slot, 64, stride=batch), :] for slot in range(batch)], axis=1
    ).astype(jnp.bfloat16)
    first = matmul(columns, k_first[...], ((0,), (0,))) * scale_one
    for slot in range(batch):
        pre_one[pl.ds(slot, 128, stride=batch), :] = first[slot * 128 : slot * 128 + 128]
    value = pre_one[...]
    hidden = (value * sigmoid(value)).astype(jnp.bfloat16).astype(jnp.float32)
    hidden3 = z_shifts(hidden.reshape(16, 8, batch, 64), 1)
    hidden_t = hidden3.T.astype(jnp.bfloat16)
    hid_pad[1:5, 1:5] = hidden3.astype(jnp.bfloat16).reshape(4, 4, 8 * batch, 192)
    total = jnp.zeros((points, 64), jnp.float32)
    for pair in range(9):
        total = total + matmul(window(hid_pad, pair // 3 - 1, pair % 3 - 1), k_second[pair])
    second = total * scale_two
    pre_two[...] = second
    act = (second * sigmoid(second)).reshape(2, 2, 2, 2, 8 * batch, 64)
    pool = (act[:, 0, :, 0] + act[:, 0, :, 1] + act[:, 1, :, 0] + act[:, 1, :, 1]) * 0.25
    pieces = pool.reshape(32, batch, 64)
    features = jnp.concatenate([pieces[i] for i in range(32)], axis=1).astype(jnp.bfloat16)
    feat_ref[...] = features
    fetch.wait()
    third = jnp.concatenate(
        [matmul(features, w_vmem[:, j * 512 : j * 512 + 512]) for j in range(4)], axis=1
    ) * scale_dense
    gate = sigmoid(third)
    hidden_three = (third * gate).astype(jnp.bfloat16).astype(jnp.float32)
    errors = []
    for i in range(2):
        pred = jnp.sum(hidden_three * w_out[i : i + 1, :], axis=1, keepdims=True) * scale_dense
        pred_ref[:, i : i + 1] = pred
        error = valid[...] * (pred - aims[:, i : i + 1])
        grad_out_ref[i : i + 1, :] = (
            jnp.sum(hidden_three * error, axis=0, keepdims=True) * scale_dense
        )
        errors.append(error)
    outer = errors[0] * w_out[0:1, :] + errors[1] * w_out[1:2, :]
    delta_three = (outer * scale_dense * (gate * (1.0 + third * (1.0 - gate)))).astype(jnp.bfloat16)
    delta_ref[...] = delta_three
    for j in range(8):
        back = matmul(delta_three, w_vmem[j * 256 : j * 256 + 256, :], ((1,), (1,)))
        for i in range(4):
            pooled[j // 2, (j % 2) * 4 + i] = back[:, i * 64 : i * 64 + 64]
    spread = (pooled[...] * (scale_dense * 0.25)).reshape(2, 1, 2, 1, 8 * batch, 64)
    spread = jnp.broadcast_to(spread, (2, 2, 2, 2, 8 * batch, 64)).reshape(points, 64)
    delta = (spread * silu_slope(pre_two[...])).astype(jnp.bfloat16).astype(jnp.float32)
    mid_pad[1:5, 1:5] = delta.astype(jnp.bfloat16).reshape(4, 4, 8 * batch, 64)
    delta3 = z_shifts(delta.reshape(16, 8, batch, 64), -1)
    del_pad[1:5, 1:5] = delta3.astype(jnp.bfloat16).reshape(4, 4, 8 * batch, 192)
    total = jnp.zeros((points, 64), jnp.float32)
    for pair in range(9):
        first_off, second_off = 1 - pair // 3, 1 - pair % 3
        grad_two_ref[pair] = (
            matmul(hidden_t, window(mid_pad, first_off, second_off)) * scale_two
        )
        total = total + matmul(
            window(del_pad, first_off, second_off), k_back[pair], ((1,), (1,))
        )
    pre_one[...] = total * scale_two * silu_slope(pre_one[...])
    delta_one = jnp.concatenate(
        [pre_one[pl.ds(slot, 128, stride=batch), :] for slot in range(batch)], axis=0
    ).astype(jnp.bfloat16)
    grad_one_ref[...] = matmul(columns, delta_one) * scale_one


def forward_back(rows, aims, valid, k_first, k_second, w_hidden, w_out):
    batch = rows.shape[0]
    k_pairs = k_second.reshape(9, 192, 64)
    k_back = k_second.reshape(9, 3, 64, 64).transpose(0, 2, 1, 3).reshape(9, 64, 192)
    vmem = pl.BlockSpec(memory_space=pltpu.VMEM)
    return pl.pallas_call(
        network,
        out_shape=(
            jax.ShapeDtypeStruct((batch, 2), jnp.float32),
            jax.ShapeDtypeStruct((64, 64), jnp.float32),
            jax.ShapeDtypeStruct((9, 192, 64), jnp.float32),
            jax.ShapeDtypeStruct((2, 2048), jnp.float32),
            jax.ShapeDtypeStruct((batch, 2048), jnp.bfloat16),
            jax.ShapeDtypeStruct((batch, 2048), jnp.bfloat16),
        ),
        in_specs=[vmem] * 6 + [pl.BlockSpec(memory_space=pl.ANY), vmem],
        out_specs=(vmem,) * 6,
        scratch_shapes=[
            pltpu.VMEM((2048, 2048), jnp.bfloat16),
            pltpu.VMEM((64 * batch, 128), jnp.float32),
            pltpu.VMEM((128 * batch, 64), jnp.float32),
            pltpu.VMEM((6, 6, 8 * batch, 192), jnp.bfloat16),
            pltpu.VMEM((6, 6, 8 * batch, 192), jnp.bfloat16),
            pltpu.VMEM((6, 6, 8 * batch, 64), jnp.bfloat16),
            pltpu.VMEM((128 * batch, 64), jnp.float32),
            pltpu.VMEM((4, 8, batch, 64), jnp.float32),
            pltpu.SemaphoreType.DMA,
        ],
        compiler_params=pltpu.CompilerParams(vmem_limit_bytes=48 * 1024 * 1024),
    )(
        rows, aims, valid, jnp.pad(k_first, ((0, 10), (0, 0))), k_pairs, k_back, w_hidden,
        w_out.T.astype(jnp.float32),
    )


def row_update(weight, grad):
    scale = jnp.sqrt(jnp.mean(grad * grad, axis=-1, keepdims=True) + rms_eps)
    return weight.astype(jnp.float32) - learn_rate * grad / scale


def whole_update(weight, grad):
    scale = jnp.sqrt(jnp.mean(grad * grad) + rms_eps)
    return weight.astype(jnp.float32) - learn_rate * grad / scale


def body(velocity, sample_block, sample_member, k_first, k_second, w_hidden, w_out):
    wall_count = lax.axis_size("wall")
    wall_place = lax.axis_index("wall")
    flow_count = lax.axis_size("stream")
    flow_place = lax.axis_index("stream")
    padded = with_halo(velocity, (("wall", 1), ("stream", 2)), 1)
    keep_low = (wall_place > 0).astype(jnp.float32)
    keep_high = (wall_place < wall_count - 1).astype(jnp.float32)
    below = padded[:, 0, 1:-1, :] * keep_low
    above = padded[:, -1, 1:-1, :] * keep_high
    left_face = padded[:, 1:-1, 0, :]
    right_face = padded[:, 1:-1, -1, :]
    size_y, size_x, size_z = (velocity.shape[1], velocity.shape[2], velocity.shape[3])
    pair_y, lift_half = axis_matrices(size_y // P_SIZE, False)
    pair_x, lift_same = axis_matrices(size_x // P_SIZE, False)
    pair_z, lift_again = axis_matrices(size_z // P_SIZE, True)
    along_y = jnp.einsum("cyxz,wy->cwxz", velocity, pair_y, precision=highest)
    grad_y = (
        along_y[:, :size_y]
        .at[:, 0]
        .add(-lift_half * below)
        .at[:, size_y - 1]
        .add(lift_half * above)
    )
    high_y = along_y[:, size_y:]
    along_x = jnp.einsum("cyxz,wx->cywz", velocity, pair_x, precision=highest)
    grad_x = (
        along_x[:, :, :size_x]
        .at[:, :, 0]
        .add(-lift_half * left_face)
        .at[:, :, size_x - 1]
        .add(lift_half * right_face)
    )
    high_x = along_x[:, :, size_x:]
    along_z = jnp.einsum("cyxz,wz->cyxw", velocity, pair_z, precision=highest)
    grad_z = along_z[..., :size_z]
    high_z = along_z[..., size_z:]
    advect = velocity[0][None] * grad_x + velocity[1][None] * grad_y + velocity[2][None] * grad_z
    new_field = velocity + time_step * (-advect - relax_rate * (high_x + high_y + high_z))
    rows_y, rows_x, rows_z = (size_y // PY, size_x // PX, size_z // PZ)
    tangent = jnp.stack([velocity[0], velocity[2]]).reshape(2, rows_y, PY, rows_x, PX, rows_z, PZ)
    blocks = tangent.transpose(1, 3, 5, 0, 2, 4, 6).reshape(-1, 2 * PY * PX * PZ)
    slope_wall = jnp.stack([grad_y[0], grad_y[2]]).reshape(2, rows_y, PY, rows_x, PX, rows_z, PZ)
    stress_true = (
        (viscosity * jnp.mean(slope_wall, axis=(2, 4, 6))).transpose(1, 2, 3, 0).reshape(-1, 2)
    )
    picked = sample_block.reshape(-1)
    members = sample_member.reshape(-1)
    patch_rows = jnp.take(blocks, picked, axis=0).astype(jnp.bfloat16)
    aim_rows = jnp.take(stress_true, picked, axis=0).astype(jnp.bfloat16)
    select = slot_matrix(members, wall_count)
    select_half = select.astype(jnp.bfloat16)
    send_rows = jnp.dot(select_half, patch_rows, preferred_element_type=jnp.float32).astype(
        jnp.bfloat16
    )
    send_aims = jnp.dot(select_half, aim_rows, preferred_element_type=jnp.float32).astype(
        jnp.bfloat16
    )
    send_valid = jnp.sum(select, axis=1).astype(jnp.bfloat16)
    parcel = jnp.concatenate(
        [send_rows, send_aims, send_valid[:, None], jnp.zeros((select.shape[0], 125), jnp.bfloat16)], axis=1
    )
    parcel = lax.all_to_all(parcel, "wall", split_axis=0, concat_axis=0, tiled=True)
    tail = parcel[:, 256:259].astype(jnp.float32)
    pred, grad_one, grad_two, grad_out, features, delta_three = forward_back(
        parcel[:, :256], tail[:, 0:2], tail[:, 2:3], k_first[0], k_second[0], w_hidden[0], w_out[0]
    )
    grad_one = grad_one[:54]
    grad_two = grad_two.reshape(27, 64, 64)
    back = lax.all_to_all(pred, "wall", split_axis=0, concat_axis=0, tiled=True)
    stress_local = jnp.dot(select.T, back, precision=highest)
    stress = stress_local.T[:, None, :]
    share_rows = FEATS // flow_count
    dense_scale = 1.0 / math.sqrt(1.0 * FEATS)
    columns_here = lax.all_to_all(features, "stream", split_axis=1, concat_axis=0, tiled=True)
    grad_hidden = (
        jnp.dot(
            columns_here.T,
            lax.all_gather(delta_three, "stream", axis=0, tiled=True),
            preferred_element_type=jnp.float32,
        )
        * dense_scale
    )
    own_rows = lax.dynamic_slice_in_dim(w_hidden[0], flow_place * share_rows, share_rows, 0)
    new_w_hidden = row_update(own_rows, grad_hidden)[None]
    grad_one, grad_two, grad_out = lax.psum((grad_one, grad_two, grad_out), "stream")
    new_k_second = row_update(k_second[0], grad_two)
    new_k_first = row_update(k_first[0], grad_one)
    new_w_out = whole_update(w_out[0], grad_out.T)
    return (new_field, stress, new_k_first[None], new_k_second[None], new_w_hidden, new_w_out[None])


def solution(mesh):
    placed = (
        P(None, "wall", "stream", None),
        P("wall", "stream"),
        P("wall", "stream", None),
        P("wall", None, None),
        P("wall", None, None, None),
        P("wall", None, None),
        P("wall", None, None),
    )
    return jax.shard_map(
        body,
        mesh=mesh,
        in_specs=placed,
        out_specs=(
            P(None, "wall", "stream", None),
            P(None, "wall", "stream"),
            P("wall", None, None),
            P("wall", None, None, None),
            P("wall", "stream", None),
            P("wall", None, None),
        ),
        check_vma=False,
    )
```

```python
import functools
import math

import jax
import jax.numpy as jnp
import numpy as np
from jax import lax
from jax.experimental import pallas as pl
from jax.experimental.pallas import tpu as pltpu
from jax.sharding import PartitionSpec as P

P_SIZE = 8
PY = 4
PX = 4
PZ = 8
CAP = 2


highest = lax.Precision.HIGHEST
time_step = 0.005
relax_rate = 20.0
viscosity = 0.3
learn_rate = 0.5
rms_eps = 1e-06
tap_offsets = [
    (first_off, second_off, third_off)
    for first_off in (-1, 0, 1)
    for second_off in (-1, 0, 1)
    for third_off in (-1, 0, 1)
]


def with_halo(shard, sides, width):
    for axis, dim in sides:
        size, length = (lax.axis_size(axis), shard.shape[dim])
        up = [(i, (i + 1) % size) for i in range(size)]
        down = [(j, i) for i, j in up]
        last = lax.slice_in_dim(shard, length - width, length, axis=dim)
        first = lax.slice_in_dim(shard, 0, width, axis=dim)
        before = lax.ppermute(last, axis, up)
        after = lax.ppermute(first, axis, down)
        shard = jnp.concatenate([before, shard, after], axis=dim)
    return shard


def cheb_tables(points):
    order = points - 1
    node_index = np.arange(points)
    nodes = -np.cos(np.pi * node_index / order)
    end_weight = np.where((node_index == 0) | (node_index == order), 2.0, 1.0)
    parity = (-1.0) ** (node_index[:, None] + node_index[None, :])
    offdiag = 1.0 - np.eye(points)
    spread = nodes[:, None] - nodes[None, :] + np.eye(points)
    deriv = end_weight[:, None] / end_weight[None, :] * parity / spread * offdiag
    deriv = deriv - np.eye(points) * deriv.sum(axis=1)[:, None]
    highpass = parity / (order * end_weight[None, :])
    return (deriv, highpass, 0.5 * order * order)


def axis_matrices(count, periodic):
    deriv, highpass, lift_half = cheb_tables(P_SIZE)
    length = count * P_SIZE
    slope = np.kron(np.eye(count), deriv)
    upper = np.kron(np.eye(count), highpass)
    faces = count if periodic else count - 1
    for element in range(faces):
        last_node = element * P_SIZE + P_SIZE - 1
        next_node = (element + 1) % count * P_SIZE
        slope[last_node, next_node] += lift_half
        slope[last_node, last_node] -= lift_half
        slope[next_node, last_node] -= lift_half
        slope[next_node, next_node] += lift_half
    if not periodic:
        slope[0, 0] += lift_half
        slope[length - 1, length - 1] -= lift_half
    paired = jnp.asarray(np.concatenate([slope, upper], axis=0), jnp.float32)
    return (paired, lift_half)


def slot_matrix(members, member_count):
    member_hot = (members[..., None] == jnp.arange(member_count, dtype=jnp.int32)).astype(jnp.int32)
    before = jnp.cumsum(member_hot, axis=-2) - member_hot
    ranks = jnp.sum(before * member_hot, axis=-1)
    slots = members * CAP + ranks
    return (slots[..., None, :] == jnp.arange(member_count * CAP, dtype=jnp.int32)[:, None]).astype(
        jnp.float32
    )


def sigmoid(value):
    return 1.0 / (1.0 + jnp.exp(-value))


def silu_slope(value):
    gate = sigmoid(value)
    return gate * (1.0 + value * (1.0 - gate))


def z_shifts(grid, sign):
    edge = jnp.zeros((16, 1, grid.shape[2], grid.shape[-1]), grid.dtype)
    before = jnp.concatenate([edge, grid[:, :-1]], axis=1)
    after = jnp.concatenate([grid[:, 1:], edge], axis=1)
    parts = [before, grid, after] if sign > 0 else [after, grid, before]
    return jnp.concatenate([part.reshape(-1, grid.shape[-1]) for part in parts], axis=-1)


def window(padded, first, second):
    return padded[1 + first : 5 + first, 1 + second : 5 + second].reshape(-1, padded.shape[-1])


def clear_border(padded):
    row = jnp.zeros((1, 6) + padded.shape[2:], padded.dtype)
    column = jnp.zeros((6, 1) + padded.shape[2:], padded.dtype)
    padded[0:1] = row
    padded[5:6] = row
    padded[:, 0:1] = column
    padded[:, 5:6] = column


def matmul(left, right, dims=((1,), (0,))):
    return lax.dot_general(left, right, (dims, ((), ())), preferred_element_type=jnp.float32)


def remote(source, target, semaphores, row, hop, axis, peer):
    return pltpu.make_async_remote_copy(
        src_ref=source, dst_ref=target,
        send_sem=semaphores.at[row, hop], recv_sem=semaphores.at[row + 1, hop],
        device_id={axis: peer}, device_id_type=pl.DeviceIdType.MESH,
    )


def head(third, w_out, tail):
    scale_dense = 1.0 / math.sqrt(2048.0)
    gate = sigmoid(third)
    hidden = (third * gate).astype(jnp.bfloat16).astype(jnp.float32)
    preds, errors, sums = [], [], []
    for i in range(2):
        pred = jnp.sum(hidden * w_out[i : i + 1, :], axis=1, keepdims=True) * scale_dense
        error = tail[:, 2:3] * (pred - tail[:, i : i + 1])
        sums.append(jnp.sum(hidden * error, axis=0, keepdims=True) * scale_dense)
        preds.append(pred)
        errors.append(error)
    outer = errors[0] * w_out[0:1, :] + errors[1] * w_out[1:2, :]
    delta = (outer * scale_dense * (gate * (1.0 + third * (1.0 - gate)))).astype(jnp.bfloat16)
    return preds, sums, delta


def network(
    n, walls, per, parcel, k_first, k_second, k_back, w_hbm, w_out,
    back_ref, new_first, new_second, new_hidden, new_out,
    w_vmem, cols, pre_one, hid_pad, del_pad, mid_pad, pre_two, pooled,
    feat_in, tail_in, feat_all, delta_all, grads, grads_in, update, pred_in,
    w_sem, sems, wall_sems,
):
    me, wall = lax.axis_index("stream"), lax.axis_index("wall")
    barrier = pltpu.get_barrier_semaphore()
    for hop in range(1, n):
        pl.semaphore_signal(
            barrier, inc=1, device_id={"stream": lax.rem(me + hop, n)},
            device_id_type=pl.DeviceIdType.MESH,
        )
    for hop in range(1, walls):
        pl.semaphore_signal(
            barrier, inc=1, device_id={"wall": lax.rem(wall + hop, walls)},
            device_id_type=pl.DeviceIdType.MESH,
        )
    batch = parcel.shape[0]
    points = 128 * batch
    share = 2048 // n
    tail = parcel[:, 256:384].astype(jnp.float32)
    rows = parcel[:, 0:256].astype(jnp.float32)
    fetch = pltpu.make_async_copy(w_hbm, w_vmem, w_sem)
    fetch.start()
    scale_one = 1.0 / math.sqrt(54.0)
    scale_two = 1.0 / math.sqrt(1728.0)
    scale_dense = 1.0 / math.sqrt(2048.0)
    clear_border(hid_pad)
    clear_border(del_pad)
    clear_border(mid_pad)
    lane = lax.broadcasted_iota(jnp.int32, (batch, 128), 1)
    at = (lane // 32, (lane // 8) % 4, lane % 8)
    cols[54 * batch : 64 * batch, :] = jnp.zeros((10 * batch, 128), jnp.float32)
    channel = [rows[:, 0:128], rows[:, 128:256]]
    for tap, offset in enumerate(tap_offsets):
        inside = None
        for place, step, size in zip(at, offset, (4, 4, 8)):
            if step:
                good = (place + step >= 0) & (place + step < size)
                inside = good if inside is None else inside & good
        turn = (-(offset[0] * 32 + offset[1] * 8 + offset[2])) % 128
        for c in range(2):
            moved = channel[c] if turn == 0 else pltpu.roll(channel[c], turn, 1)
            if inside is not None:
                moved = jnp.where(inside, moved, 0.0)
            cols[(2 * tap + c) * batch : (2 * tap + c + 1) * batch, :] = moved
    columns = jnp.concatenate(
        [cols[pl.ds(slot, 64, stride=batch), :] for slot in range(batch)], axis=1
    ).astype(jnp.bfloat16)
    first = matmul(columns, k_first[...], ((0,), (0,))) * scale_one
    for slot in range(batch):
        pre_one[pl.ds(slot, 128, stride=batch), :] = first[slot * 128 : slot * 128 + 128]
    value = pre_one[...]
    hidden = (value * sigmoid(value)).astype(jnp.bfloat16).astype(jnp.float32)
    hidden3 = z_shifts(hidden.reshape(16, 8, batch, 64), 1)
    hidden_t = hidden3.T.astype(jnp.bfloat16)
    hid_pad[1:5, 1:5] = hidden3.astype(jnp.bfloat16).reshape(4, 4, 8 * batch, 192)
    total = jnp.zeros((points, 64), jnp.float32)
    for pair in range(9):
        total = total + matmul(window(hid_pad, pair // 3 - 1, pair % 3 - 1), k_second[pair * 192 : pair * 192 + 192, :])
    second = total * scale_two
    pre_two[...] = second
    act = (second * sigmoid(second)).reshape(2, 2, 2, 2, 8 * batch, 64)
    pool = (act[:, 0, :, 0] + act[:, 0, :, 1] + act[:, 1, :, 0] + act[:, 1, :, 1]) * 0.25
    pieces = pool.reshape(32, batch, 64)
    features = jnp.concatenate([pieces[i] for i in range(32)], axis=1)
    feat_in[0] = jnp.concatenate([features[:, :1024], features[:, 1024:]], axis=0).astype(
        jnp.bfloat16
    )
    tail_in[0] = tail
    features = features.astype(jnp.bfloat16)
    pl.semaphore_wait(barrier, n + walls - 2)
    copies = []
    for hop in range(1, n):
        peer = lax.rem(me + hop, n)
        copies.append(remote(feat_in.at[0], feat_in.at[hop], sems, 0, hop, "stream", peer))
        copies.append(remote(tail_in.at[0], tail_in.at[hop], sems, 2, hop, "stream", peer))
    for copy in copies:
        copy.start()
    fetch.wait()

    def dense(values):
        return jnp.concatenate(
            [matmul(values, w_vmem[:, j * 512 : j * 512 + 512]) for j in range(4)], axis=1
        ) * scale_dense

    preds, _, delta_three = head(dense(features), w_out, tail)
    lane_out = lax.broadcasted_iota(jnp.int32, (batch, 128), 1)
    pred_in[0] = jnp.where(lane_out == 0, preds[0], jnp.where(lane_out == 1, preds[1], 0.0))
    returns = []
    for hop in range(1, walls):
        peer = lax.rem(wall + hop, walls)
        returns.append(remote(pred_in.at[0], pred_in.at[hop], wall_sems, 0, hop, "wall", peer))
    for copy in returns:
        copy.start()
    for j in range(8):
        back = matmul(delta_three, w_vmem[j * 256 : j * 256 + 256, :], ((1,), (1,)))
        for i in range(4):
            pooled[j // 2, (j % 2) * 4 + i] = back[:, i * 64 : i * 64 + 64]
    spread = (pooled[...] * (scale_dense * 0.25)).reshape(2, 1, 2, 1, 8 * batch, 64)
    spread = jnp.broadcast_to(spread, (2, 2, 2, 2, 8 * batch, 64)).reshape(points, 64)
    delta = (spread * silu_slope(pre_two[...])).astype(jnp.bfloat16).astype(jnp.float32)
    mid_pad[1:5, 1:5] = delta.astype(jnp.bfloat16).reshape(4, 4, 8 * batch, 64)
    delta3 = z_shifts(delta.reshape(16, 8, batch, 64), -1)
    del_pad[1:5, 1:5] = delta3.astype(jnp.bfloat16).reshape(4, 4, 8 * batch, 192)
    total = jnp.zeros((points, 64), jnp.float32)
    for pair in range(9):
        first_off, second_off = 1 - pair // 3, 1 - pair % 3
        grad_two = (matmul(hidden_t, window(mid_pad, first_off, second_off)) * scale_two).astype(
            jnp.bfloat16
        )
        start = pair * 192
        if start + 192 <= 896:
            grads[start : start + 192, 0:64] = grad_two
        elif start >= 896:
            grads[start - 896 : start - 704, 64:128] = grad_two
        else:
            grads[start:896, 0:64] = grad_two[: 896 - start]
            grads[0 : start - 704, 64:128] = grad_two[896 - start :]
        total = total + matmul(
            window(del_pad, first_off, second_off), k_back[pair], ((1,), (1,))
        )
    pre_one[...] = total * scale_two * silu_slope(pre_one[...])
    delta_one = jnp.concatenate(
        [pre_one[pl.ds(slot, 128, stride=batch), :] for slot in range(batch)], axis=0
    ).astype(jnp.bfloat16)
    grads[832:896, 64:128] = (matmul(columns, delta_one) * scale_one).astype(jnp.bfloat16)
    if n * per > 896:
        grads[896 : n * per, :] = jnp.zeros((n * per - 896, 128), jnp.bfloat16)
    scatter = []
    for hop in range(1, n):
        peer = lax.rem(me + hop, n)
        chunk = grads.at[pl.ds(pl.multiple_of(peer * per, 16), per)]
        scatter.append(remote(chunk, grads_in.at[hop], sems, 4, hop, "stream", peer))
    for copy in scatter:
        copy.start()

    for copy in copies:
        copy.wait_recv()
    for hop in range(n):
        pair = feat_in[hop].astype(jnp.float32)
        feat_all[hop * batch : hop * batch + batch, 0:1024] = pair[:batch]
        feat_all[hop * batch : hop * batch + batch, 1024:2048] = pair[batch:]
    grad_out = [jnp.zeros((1, 2048), jnp.float32), jnp.zeros((1, 2048), jnp.float32)]
    group = 64 // batch
    for part in range(n // group):
        span = slice(part * 64, part * 64 + 64)
        tails = tail_in[part * group : part * group + group].reshape(64, 128)
        _, sums, delta_part = head(dense(feat_all[span, :].astype(jnp.bfloat16)), w_out, tails)
        delta_all[span, :] = delta_part
        grad_out = [old + new for old, new in zip(grad_out, sums)]
    square = (jnp.sum(grad_out[0] * grad_out[0]) + jnp.sum(grad_out[1] * grad_out[1])) / 4096.0
    for i in range(2):
        new_out[i : i + 1, :] = w_out[i : i + 1, :] - learn_rate * grad_out[i] * lax.rsqrt(
            square + rms_eps
        )

    total = grads[pl.ds(pl.multiple_of(me * per, 16), per), :].astype(jnp.float32)
    for hop in range(1, n):
        scatter[hop - 1].wait_recv()
        total = total + grads_in[hop].astype(jnp.float32)
    left = jnp.mean(total[:, :64] * total[:, :64], axis=1, keepdims=True) + rms_eps
    right = jnp.mean(total[:, 64:] * total[:, 64:], axis=1, keepdims=True) + rms_eps
    lane_all = lax.broadcasted_iota(jnp.int32, (per, 128), 1)
    update[me] = (total * jnp.where(lane_all < 64, lax.rsqrt(left), lax.rsqrt(right))).astype(
        jnp.bfloat16
    )
    gather = []
    for hop in range(1, n):
        peer = lax.rem(me + hop, n)
        gather.append(remote(update.at[me], update.at[me], sems, 6, hop, "stream", peer))
    for copy in gather:
        copy.start()

    if share % 128 == 0:
        own_feat = feat_all[:, pl.ds(pl.multiple_of(me * share, 128), share)]
    else:
        picks = lax.broadcasted_iota(jnp.int32, (2048, share), 0) - me * share
        hot = picks == lax.broadcasted_iota(jnp.int32, (2048, share), 1)
        own_feat = matmul(feat_all[...].astype(jnp.bfloat16), jnp.where(hot, 1.0, 0.0).astype(jnp.bfloat16))
    own_feat = own_feat.T.astype(jnp.bfloat16)
    for part in range(share // 64):
        grad = matmul(own_feat[part * 64 : part * 64 + 64], delta_all[...]) * scale_dense
        rate = learn_rate * lax.rsqrt(jnp.mean(grad * grad, axis=1, keepdims=True) + rms_eps)
        weight = w_vmem[pl.ds(pl.multiple_of(me * share + part * 64, 64), 64), :]
        new_hidden[part * 64 : part * 64 + 64, :] = weight.astype(jnp.float32) - grad * rate

    for copy in returns:
        copy.wait_recv()
    back_ref[...] = pred_in[...]
    for copy in gather:
        copy.wait_recv()
    step = update[...].reshape(n * per, 128).astype(jnp.float32) * learn_rate
    new_second[0:896, :] = k_second[0:896, :].astype(jnp.float32) - step[:896, :64]
    new_second[896:1728, :] = k_second[896:1728, :].astype(jnp.float32) - step[:832, 64:]
    new_first[...] = k_first[...].astype(jnp.float32) - step[832:896, 64:]
    for copy in copies + returns + scatter + gather:
        copy.wait_send()


def train(parcel, k_first, k_second, w_hidden, w_out):
    batch = parcel.shape[0]
    n, walls = lax.axis_size("stream"), lax.axis_size("wall")
    per = -(-896 // (n * 16)) * 16
    k_back = k_second.reshape(9, 3, 64, 64).transpose(0, 2, 1, 3).reshape(9, 64, 192)
    vmem = pl.BlockSpec(memory_space=pltpu.VMEM)
    return pl.pallas_call(
        functools.partial(network, n, walls, per),
        out_shape=(
            jax.ShapeDtypeStruct((walls, batch, 128), jnp.float32),
            jax.ShapeDtypeStruct((64, 64), jnp.float32),
            jax.ShapeDtypeStruct((1728, 64), jnp.float32),
            jax.ShapeDtypeStruct((2048 // n, 2048), jnp.float32),
            jax.ShapeDtypeStruct((2, 2048), jnp.float32),
        ),
        in_specs=[vmem] * 4 + [pl.BlockSpec(memory_space=pl.ANY), vmem],
        out_specs=(vmem,) * 5,
        scratch_shapes=[
            pltpu.VMEM((2048, 2048), jnp.bfloat16),
            pltpu.VMEM((64 * batch, 128), jnp.float32),
            pltpu.VMEM((128 * batch, 64), jnp.float32),
            pltpu.VMEM((6, 6, 8 * batch, 192), jnp.bfloat16),
            pltpu.VMEM((6, 6, 8 * batch, 192), jnp.bfloat16),
            pltpu.VMEM((6, 6, 8 * batch, 64), jnp.bfloat16),
            pltpu.VMEM((128 * batch, 64), jnp.float32),
            pltpu.VMEM((4, 8, batch, 64), jnp.float32),
            pltpu.VMEM((n, 2 * batch, 1024), jnp.bfloat16),
            pltpu.VMEM((n, batch, 128), jnp.float32),
            pltpu.VMEM((n * batch, 2048), jnp.float32),
            pltpu.VMEM((n * batch, 2048), jnp.bfloat16),
            pltpu.VMEM((n * per, 128), jnp.bfloat16),
            pltpu.VMEM((n, per, 128), jnp.bfloat16),
            pltpu.VMEM((n, per, 128), jnp.bfloat16),
            pltpu.VMEM((walls, batch, 128), jnp.float32),
            pltpu.SemaphoreType.DMA,
            pltpu.SemaphoreType.DMA((8, n)),
            pltpu.SemaphoreType.DMA((2, walls)),
        ],
        compiler_params=pltpu.CompilerParams(
            vmem_limit_bytes=52 * 1024 * 1024, collective_id=0, has_side_effects=True
        ),
    )(
        parcel, jnp.pad(k_first, ((0, 10), (0, 0))), k_second.reshape(1728, 64), k_back, w_hidden,
        w_out.T.astype(jnp.float32),
    )


def body(velocity, sample_block, sample_member, k_first, k_second, w_hidden, w_out):
    wall_count = lax.axis_size("wall")
    wall_place = lax.axis_index("wall")
    padded = with_halo(velocity, (("wall", 1), ("stream", 2)), 1)
    keep_low = (wall_place > 0).astype(jnp.float32)
    keep_high = (wall_place < wall_count - 1).astype(jnp.float32)
    below = padded[:, 0, 1:-1, :] * keep_low
    above = padded[:, -1, 1:-1, :] * keep_high
    left_face = padded[:, 1:-1, 0, :]
    right_face = padded[:, 1:-1, -1, :]
    size_y, size_x, size_z = (velocity.shape[1], velocity.shape[2], velocity.shape[3])
    pair_y, lift_half = axis_matrices(size_y // P_SIZE, False)
    pair_x, lift_same = axis_matrices(size_x // P_SIZE, False)
    pair_z, lift_again = axis_matrices(size_z // P_SIZE, True)
    along_y = jnp.einsum("cyxz,wy->cwxz", velocity, pair_y, precision=highest)
    grad_y = (
        along_y[:, :size_y]
        .at[:, 0]
        .add(-lift_half * below)
        .at[:, size_y - 1]
        .add(lift_half * above)
    )
    high_y = along_y[:, size_y:]
    along_x = jnp.einsum("cyxz,wx->cywz", velocity, pair_x, precision=highest)
    grad_x = (
        along_x[:, :, :size_x]
        .at[:, :, 0]
        .add(-lift_half * left_face)
        .at[:, :, size_x - 1]
        .add(lift_half * right_face)
    )
    high_x = along_x[:, :, size_x:]
    along_z = jnp.einsum("cyxz,wz->cyxw", velocity, pair_z, precision=highest)
    grad_z = along_z[..., :size_z]
    high_z = along_z[..., size_z:]
    advect = velocity[0][None] * grad_x + velocity[1][None] * grad_y + velocity[2][None] * grad_z
    new_field = velocity + time_step * (-advect - relax_rate * (high_x + high_y + high_z))
    rows_y, rows_x, rows_z = (size_y // PY, size_x // PX, size_z // PZ)
    tangent = jnp.stack([velocity[0], velocity[2]]).reshape(2, rows_y, PY, rows_x, PX, rows_z, PZ)
    blocks = tangent.transpose(1, 3, 5, 0, 2, 4, 6).reshape(-1, 2 * PY * PX * PZ)
    slope_wall = jnp.stack([grad_y[0], grad_y[2]]).reshape(2, rows_y, PY, rows_x, PX, rows_z, PZ)
    stress_true = (
        (viscosity * jnp.mean(slope_wall, axis=(2, 4, 6))).transpose(1, 2, 3, 0).reshape(-1, 2)
    )
    picked = sample_block.reshape(-1)
    members = sample_member.reshape(-1)
    patch_rows = jnp.take(blocks, picked, axis=0).astype(jnp.bfloat16)
    aim_rows = jnp.take(stress_true, picked, axis=0).astype(jnp.bfloat16)
    select = slot_matrix(members, wall_count)
    select_half = select.astype(jnp.bfloat16)
    send_rows = jnp.dot(select_half, patch_rows, preferred_element_type=jnp.float32).astype(
        jnp.bfloat16
    )
    send_aims = jnp.dot(select_half, aim_rows, preferred_element_type=jnp.float32).astype(
        jnp.bfloat16
    )
    send_valid = jnp.sum(select, axis=1).astype(jnp.bfloat16)
    parcel = jnp.concatenate(
        [send_rows, send_aims, send_valid[:, None], jnp.zeros((select.shape[0], 125), jnp.bfloat16)], axis=1
    )
    parcel = lax.all_to_all(parcel, "wall", split_axis=0, concat_axis=0, tiled=True)
    gathered, new_first, new_second, new_w_hidden, new_out = train(
        parcel, k_first[0], k_second[0], w_hidden[0], w_out[0]
    )
    mine = lax.dynamic_slice_in_dim(gathered[:, :, :2], wall_place * CAP, CAP, 1)
    source = (wall_place - jnp.arange(wall_count)) % wall_count
    order = (source[None, :] == jnp.arange(wall_count)[:, None]).astype(jnp.float32)
    back = jnp.einsum("ph,hrk->prk", order, mine, precision=highest).reshape(-1, 2)
    stress_local = jnp.dot(select.T, back, precision=highest)
    stress = stress_local.T[:, None, :]
    return (
        new_field, stress, new_first[None, :54], new_second.reshape(k_second.shape),
        new_w_hidden[None], new_out.T[None],
    )


def solution(mesh):
    placed = (
        P(None, "wall", "stream", None),
        P("wall", "stream"),
        P("wall", "stream", None),
        P("wall", None, None),
        P("wall", None, None, None),
        P("wall", None, None),
        P("wall", None, None),
    )
    return jax.shard_map(
        body,
        mesh=mesh,
        in_specs=placed,
        out_specs=(
            P(None, "wall", "stream", None),
            P(None, "wall", "stream"),
            P("wall", None, None),
            P("wall", None, None, None),
            P("wall", "stream", None),
            P("wall", None, None),
        ),
        check_vma=False,
    )
```

```python
import functools
import math

import jax
import jax.numpy as jnp
import numpy as np
from jax import lax
from jax.experimental import pallas as pl
from jax.experimental.pallas import tpu as pltpu
from jax.sharding import PartitionSpec as P

P_SIZE = 8
CAP = 2


highest = lax.Precision.HIGHEST
time_step = 0.005
relax_rate = 20.0
viscosity = 0.3
learn_rate = 0.5
rms_eps = 1e-06
tap_offsets = [
    (first_off, second_off, third_off)
    for first_off in (-1, 0, 1)
    for second_off in (-1, 0, 1)
    for third_off in (-1, 0, 1)
]


def cheb_tables(points):
    order = points - 1
    node_index = np.arange(points)
    nodes = -np.cos(np.pi * node_index / order)
    end_weight = np.where((node_index == 0) | (node_index == order), 2.0, 1.0)
    parity = (-1.0) ** (node_index[:, None] + node_index[None, :])
    offdiag = 1.0 - np.eye(points)
    spread = nodes[:, None] - nodes[None, :] + np.eye(points)
    deriv = end_weight[:, None] / end_weight[None, :] * parity / spread * offdiag
    deriv = deriv - np.eye(points) * deriv.sum(axis=1)[:, None]
    highpass = parity / (order * end_weight[None, :])
    return (deriv, highpass, 0.5 * order * order)


def element_tables():
    slope, upper, lift = cheb_tables(P_SIZE)
    slope[0, 0] += lift
    slope[7, 7] -= lift
    return slope, upper, lift


def axis_matrix(count, slope, lift):
    whole = np.kron(np.eye(count), slope)
    for element in range(count):
        last_node = element * P_SIZE + P_SIZE - 1
        next_node = (element + 1) % count * P_SIZE
        whole[last_node, next_node] += lift
        whole[next_node, last_node] -= lift
    return whole


def sigmoid(value):
    return 1.0 / (1.0 + jnp.exp(-value))


def silu_slope(value):
    gate = sigmoid(value)
    return gate * (1.0 + value * (1.0 - gate))


def z_shifts(grid, sign):
    edge = jnp.zeros((16, 1, grid.shape[2], grid.shape[-1]), grid.dtype)
    before = jnp.concatenate([edge, grid[:, :-1]], axis=1)
    after = jnp.concatenate([grid[:, 1:], edge], axis=1)
    parts = [before, grid, after] if sign > 0 else [after, grid, before]
    return jnp.concatenate([part.reshape(-1, grid.shape[-1]) for part in parts], axis=-1)


def window(padded, first, second):
    return padded[1 + first : 5 + first, 1 + second : 5 + second].reshape(-1, padded.shape[-1])


def clear_border(padded):
    row = jnp.zeros((1, 6) + padded.shape[2:], padded.dtype)
    column = jnp.zeros((6, 1) + padded.shape[2:], padded.dtype)
    padded[0:1] = row
    padded[5:6] = row
    padded[:, 0:1] = column
    padded[:, 5:6] = column


def matmul(left, right, dims=((1,), (0,))):
    return lax.dot_general(left, right, (dims, ((), ())), preferred_element_type=jnp.float32)


def remote(source, target, semaphores, row, hop, axis, peer):
    return pltpu.make_async_remote_copy(
        src_ref=source, dst_ref=target,
        send_sem=semaphores.at[row, hop], recv_sem=semaphores.at[row + 1, hop],
        device_id={axis: peer}, device_id_type=pl.DeviceIdType.MESH,
    )


def head(third, w_out, tail):
    scale_dense = 1.0 / math.sqrt(2048.0)
    gate = sigmoid(third)
    hidden = (third * gate).astype(jnp.bfloat16).astype(jnp.float32)
    preds, errors, sums = [], [], []
    for i in range(2):
        pred = jnp.sum(hidden * w_out[i : i + 1, :], axis=1, keepdims=True) * scale_dense
        error = tail[:, 2:3] * (pred - tail[:, i : i + 1])
        sums.append(jnp.sum(hidden * error, axis=0, keepdims=True) * scale_dense)
        preds.append(pred)
        errors.append(error)
    outer = errors[0] * w_out[0:1, :] + errors[1] * w_out[1:2, :]
    delta = (outer * scale_dense * (gate * (1.0 + third * (1.0 - gate)))).astype(jnp.bfloat16)
    return preds, sums, delta


def network(
    n, walls, per, blocks, members, field, tab_x, tab_z, k_first, k_second, k_back, w_hbm, w_out,
    new_field, stress, new_first, new_second, new_hidden, new_out,
    patch_out, tail_out, w_vmem, cols, pre_one, hid_pad, del_pad, mid_pad, pre_two, pooled,
    feat_in, tail_in, feat_all, delta_all, grads, grads_in, update, pred_in,
    patch_in, tail_wall, rows_all, tails_all, face_y, face_x, edge_x,
    w_sem, sems, wall_sems, face_sems,
):
    me, wall = lax.axis_index("stream"), lax.axis_index("wall")
    barrier = pltpu.get_barrier_semaphore()
    for hop in range(1, n):
        pl.semaphore_signal(
            barrier, inc=1, device_id={"stream": lax.rem(me + hop, n)},
            device_id_type=pl.DeviceIdType.MESH,
        )
    for hop in range(1, walls):
        pl.semaphore_signal(
            barrier, inc=1, device_id={"wall": lax.rem(wall + hop, walls)},
            device_id_type=pl.DeviceIdType.MESH,
        )
    batch = 2 * walls
    points = 128 * batch
    share = 2048 // n
    samples = blocks.shape[1]
    fetch = pltpu.make_async_copy(w_hbm, w_vmem, w_sem)
    fetch.start()
    slope, upper, lift = element_tables()
    scale_one = 1.0 / math.sqrt(54.0)
    scale_two = 1.0 / math.sqrt(1728.0)
    scale_dense = 1.0 / math.sqrt(2048.0)
    clear_border(hid_pad)
    clear_border(del_pad)
    clear_border(mid_pad)
    lane = lax.broadcasted_iota(jnp.int32, (batch, 128), 1)
    at = (lane // 32, (lane // 8) % 4, lane % 8)
    cols[54 * batch : 64 * batch, :] = jnp.zeros((10 * batch, 128), jnp.float32)
    names = [members[0, k] for k in range(samples)]
    picks = [blocks[0, k] for k in range(samples)]
    ranks = []
    for k in range(samples):
        rank = jnp.int32(0)
        for j in range(k):
            rank = rank + jnp.where(names[j] == names[k], 1, 0)
        ranks.append(rank)
    hops = [lax.rem(name + walls - wall, walls) for name in names]

    def by_slot(shape):
        slot = lax.broadcasted_iota(jnp.int32, shape, 0) % batch
        found = jnp.full(shape, -1, jnp.int32)
        for k in range(samples):
            found = jnp.where(slot == hops[k] * 2 + ranks[k], picks[k], found)
        return found

    wide = (16 * batch, 128)
    found = by_slot(wide)
    point = lax.broadcasted_iota(jnp.int32, wide, 0) // batch
    lane_w = lax.broadcasted_iota(jnp.int32, wide, 1)
    row_at = ((found >> 6) * 4 + point // 4) * 16 + ((found >> 4) & 3) * 4 + point % 4
    row_hot = jnp.where((found >= 0) & (lane_w == row_at), 1.0, 0.0).astype(jnp.bfloat16)
    fold = jnp.where(
        lax.broadcasted_iota(jnp.int32, (128, 128), 0) % 8
        == lax.broadcasted_iota(jnp.int32, (128, 128), 1) % 8, 1.0, 0.0
    ).astype(jnp.bfloat16)
    for c in range(2):
        near = matmul(row_hot, field[2 * c].reshape(128, 128).astype(jnp.bfloat16))
        near = jnp.where(lane_w // 8 == (found & 15), near, 0.0).astype(jnp.bfloat16)
        folded = jnp.where(lane_w // 8 == point, matmul(near, fold), 0.0)
        folded = jnp.sum(folded.reshape(16, batch, 128), axis=0)
        rows_all[:, c * 128 : c * 128 + 128] = folded
    for hop in range(walls):
        patch_out[hop] = jnp.zeros((8, 256), jnp.float32)
        patch_out[hop, 0:2, :] = rows_all[2 * hop : 2 * hop + 2, :]
    edge_x[0] = field[:, :, 15, :]
    edge_x[1] = field[:, :, 0, :]
    pl.semaphore_wait(barrier, n + walls - 2)
    patches = []
    for hop in range(1, walls):
        peer = lax.rem(wall + hop, walls)
        patches.append(
            remote(patch_out.at[hop], patch_in.at[hop], wall_sems, 2, hop, "wall", peer)
        )
    above, below = lax.rem(wall + 1, walls), lax.rem(wall + walls - 1, walls)
    ahead, behind = lax.rem(me + 1, n), lax.rem(me + n - 1, n)
    faces_y = [
        remote(field.at[:, 7], face_y.at[0], face_sems, 0, 0, "wall", above),
        remote(field.at[:, 0], face_y.at[1], face_sems, 0, 1, "wall", below),
    ]
    faces_x = [
        remote(edge_x.at[0], face_x.at[0], face_sems, 2, 0, "stream", ahead),
        remote(edge_x.at[1], face_x.at[1], face_sems, 2, 1, "stream", behind),
    ]
    for copy in patches + faces_y + faces_x:
        copy.start()

    for copy in faces_y:
        copy.wait_recv()
    keep_low = jnp.where(wall > 0, lift, 0.0)
    keep_high = jnp.where(wall < walls - 1, lift, 0.0)
    found = by_slot((batch, 128))
    tail = jnp.where(lane == 2, jnp.where(found >= 0, 1.0, 0.0), 0.0)
    for i in range(2):
        halves = []
        for half in range(2):
            total = -keep_low * face_y[0, 2 * i] if half == 0 else keep_high * face_y[1, 2 * i]
            for j in range(8):
                weight = float(sum(slope[half * 4 : half * 4 + 4, j]))
                total = total + weight * field[2 * i, j]
            halves.append(total)
        mean = jnp.zeros((batch, 128), jnp.float32)
        for row in range(8):
            strip = halves[row // 4][row % 4 * 4 : row % 4 * 4 + 4, :]
            strip = jnp.sum(strip, axis=0, keepdims=True)
            mean = mean + jnp.where((found >> 4) == row, strip, 0.0)
        mean = jnp.where(lane // 8 == (found & 15), mean, 0.0)
        aim = jnp.sum(mean, axis=1, keepdims=True) * (viscosity / 128.0)
        tail = jnp.where((lane == i) & (found >= 0), aim.astype(jnp.bfloat16).astype(jnp.float32), tail)
    tails_all[...] = tail
    for hop in range(walls):
        tail_out[hop] = jnp.zeros((8, 128), jnp.float32)
        tail_out[hop, 0:2, :] = tails_all[2 * hop : 2 * hop + 2, :]
    targets = []
    for hop in range(1, walls):
        peer = lax.rem(wall + hop, walls)
        targets.append(
            remote(tail_out.at[hop], tail_wall.at[hop], wall_sems, 4, hop, "wall", peer)
        )
    for copy in targets:
        copy.start()

    for copy in patches:
        copy.wait_recv()
    for hop in range(1, walls):
        rows_all[2 * hop : 2 * hop + 2, :] = patch_in[hop, 0:2, :]
    channel = [rows_all[:, 0:128], rows_all[:, 128:256]]
    for tap, offset in enumerate(tap_offsets):
        inside = None
        for place, step, size in zip(at, offset, (4, 4, 8)):
            if step:
                good = (place + step >= 0) & (place + step < size)
                inside = good if inside is None else inside & good
        turn = (-(offset[0] * 32 + offset[1] * 8 + offset[2])) % 128
        for c in range(2):
            moved = channel[c] if turn == 0 else pltpu.roll(channel[c], turn, 1)
            if inside is not None:
                moved = jnp.where(inside, moved, 0.0)
            cols[(2 * tap + c) * batch : (2 * tap + c + 1) * batch, :] = moved
    columns = jnp.concatenate(
        [cols[pl.ds(slot, 64, stride=batch), :] for slot in range(batch)], axis=1
    ).astype(jnp.bfloat16)
    first = matmul(columns, k_first[...], ((0,), (0,))) * scale_one
    for slot in range(batch):
        pre_one[pl.ds(slot, 128, stride=batch), :] = first[slot * 128 : slot * 128 + 128]
    value = pre_one[...]
    hidden = (value * sigmoid(value)).astype(jnp.bfloat16).astype(jnp.float32)
    hidden3 = z_shifts(hidden.reshape(16, 8, batch, 64), 1)
    hidden_t = hidden3.T.astype(jnp.bfloat16)
    hid_pad[1:5, 1:5] = hidden3.astype(jnp.bfloat16).reshape(4, 4, 8 * batch, 192)
    total = jnp.zeros((points, 64), jnp.float32)
    for pair in range(9):
        total = total + matmul(window(hid_pad, pair // 3 - 1, pair % 3 - 1), k_second[pair * 192 : pair * 192 + 192, :])
    second = total * scale_two
    pre_two[...] = second
    act = (second * sigmoid(second)).reshape(2, 2, 2, 2, 8 * batch, 64)
    pool = (act[:, 0, :, 0] + act[:, 0, :, 1] + act[:, 1, :, 0] + act[:, 1, :, 1]) * 0.25
    pieces = pool.reshape(32, batch, 64)
    features = jnp.concatenate([pieces[i] for i in range(32)], axis=1)
    feat_in[0] = jnp.concatenate([features[:, :1024], features[:, 1024:]], axis=0).astype(
        jnp.bfloat16
    )
    for copy in targets:
        copy.wait_recv()
    for hop in range(1, walls):
        tails_all[2 * hop : 2 * hop + 2, :] = tail_wall[hop, 0:2, :]
    tail = tails_all[...]
    tail_in[0] = tail
    features = features.astype(jnp.bfloat16)
    copies = []
    for hop in range(1, n):
        peer = lax.rem(me + hop, n)
        copies.append(remote(feat_in.at[0], feat_in.at[hop], sems, 0, hop, "stream", peer))
        copies.append(remote(tail_in.at[0], tail_in.at[hop], sems, 2, hop, "stream", peer))
    for copy in copies:
        copy.start()
    fetch.wait()

    def dense(values):
        return jnp.concatenate(
            [matmul(values, w_vmem[:, j * 512 : j * 512 + 512]) for j in range(4)], axis=1
        ) * scale_dense

    preds, _, delta_three = head(dense(features), w_out, tail)
    lane_out = lax.broadcasted_iota(jnp.int32, (batch, 128), 1)
    pred_in[0] = jnp.where(lane_out == 0, preds[0], jnp.where(lane_out == 1, preds[1], 0.0))
    returns = []
    for hop in range(1, walls):
        peer = lax.rem(wall + hop, walls)
        returns.append(remote(pred_in.at[0], pred_in.at[hop], wall_sems, 0, hop, "wall", peer))
    for copy in returns:
        copy.start()
    for j in range(8):
        back = matmul(delta_three, w_vmem[j * 256 : j * 256 + 256, :], ((1,), (1,)))
        for i in range(4):
            pooled[j // 2, (j % 2) * 4 + i] = back[:, i * 64 : i * 64 + 64]
    spread = (pooled[...] * (scale_dense * 0.25)).reshape(2, 1, 2, 1, 8 * batch, 64)
    spread = jnp.broadcast_to(spread, (2, 2, 2, 2, 8 * batch, 64)).reshape(points, 64)
    delta = (spread * silu_slope(pre_two[...])).astype(jnp.bfloat16).astype(jnp.float32)
    mid_pad[1:5, 1:5] = delta.astype(jnp.bfloat16).reshape(4, 4, 8 * batch, 64)
    delta3 = z_shifts(delta.reshape(16, 8, batch, 64), -1)
    del_pad[1:5, 1:5] = delta3.astype(jnp.bfloat16).reshape(4, 4, 8 * batch, 192)
    total = jnp.zeros((points, 64), jnp.float32)
    for pair in range(9):
        first_off, second_off = 1 - pair // 3, 1 - pair % 3
        grad_two = (matmul(hidden_t, window(mid_pad, first_off, second_off)) * scale_two).astype(
            jnp.bfloat16
        )
        start = pair * 192
        if start + 192 <= 896:
            grads[start : start + 192, 0:64] = grad_two
        elif start >= 896:
            grads[start - 896 : start - 704, 64:128] = grad_two
        else:
            grads[start:896, 0:64] = grad_two[: 896 - start]
            grads[0 : start - 704, 64:128] = grad_two[896 - start :]
        total = total + matmul(
            window(del_pad, first_off, second_off), k_back[pair], ((1,), (1,))
        )
    pre_one[...] = total * scale_two * silu_slope(pre_one[...])
    delta_one = jnp.concatenate(
        [pre_one[pl.ds(slot, 128, stride=batch), :] for slot in range(batch)], axis=0
    ).astype(jnp.bfloat16)
    grads[832:896, 64:128] = (matmul(columns, delta_one) * scale_one).astype(jnp.bfloat16)
    if n * per > 896:
        grads[896 : n * per, :] = jnp.zeros((n * per - 896, 128), jnp.bfloat16)
    scatter = []
    for hop in range(1, n):
        peer = lax.rem(me + hop, n)
        chunk = grads.at[pl.ds(pl.multiple_of(peer * per, 16), per)]
        scatter.append(remote(chunk, grads_in.at[hop], sems, 4, hop, "stream", peer))
    for copy in scatter:
        copy.start()

    for copy in faces_x:
        copy.wait_recv()
    flow = field[...]
    split = flow.reshape(3, 8, 2, 8, 128)
    grad_x = jnp.zeros((3, 8, 2, 8, 128), jnp.float32)
    high = jnp.zeros((3, 8, 2, 8, 128), jnp.float32)
    for j in range(8):
        spread_j = split[:, :, :, j : j + 1, :]
        grad_x = grad_x + tab_x[0, j] * spread_j
        high = high + tab_x[1, j] * spread_j
    left_side = jnp.concatenate([face_x[0][:, :, None], split[:, :, 0:1, 7]], axis=2)[:, :, :, None]
    right_side = jnp.concatenate([split[:, :, 1:2, 0], face_x[1][:, :, None]], axis=2)[:, :, :, None]
    node = lax.broadcasted_iota(jnp.int32, (1, 1, 1, 8, 128), 3)
    grad_x = grad_x - jnp.where(node == 0, lift * left_side, 0.0)
    grad_x = grad_x + jnp.where(node == 7, lift * right_side, 0.0)
    grad_x = grad_x.reshape(3, 8, 16, 128)
    high = high.reshape(3, 8, 16, 128)
    along = lax.dot_general(
        flow.reshape(384, 128), tab_z[...], (((1,), (0,)), ((), ())),
        precision=highest, preferred_element_type=jnp.float32,
    )
    grad_z = along[:, :128].reshape(3, 8, 16, 128)
    high = high + along[:, 128:].reshape(3, 8, 16, 128)
    for i in range(8):
        grad_y = float(slope[i, 0]) * flow[:, 0]
        high_i = high[:, i] + float(upper[i, 0]) * flow[:, 0]
        for j in range(1, 8):
            grad_y = grad_y + float(slope[i, j]) * flow[:, j]
            high_i = high_i + float(upper[i, j]) * flow[:, j]
        if i == 0:
            grad_y = grad_y - keep_low * face_y[0]
        if i == 7:
            grad_y = grad_y + keep_high * face_y[1]
        advect = flow[0:1, i] * grad_x[:, i] + flow[1:2, i] * grad_y + flow[2:3, i] * grad_z[:, i]
        new_field[:, i] = flow[:, i] + time_step * (-advect - relax_rate * high_i)

    for copy in copies:
        copy.wait_recv()
    for hop in range(n):
        pair = feat_in[hop].astype(jnp.float32)
        feat_all[hop * batch : hop * batch + batch, 0:1024] = pair[:batch]
        feat_all[hop * batch : hop * batch + batch, 1024:2048] = pair[batch:]
    grad_out = [jnp.zeros((1, 2048), jnp.float32), jnp.zeros((1, 2048), jnp.float32)]
    group = 64 // batch
    for part in range(n // group):
        span = slice(part * 64, part * 64 + 64)
        tails = tail_in[part * group : part * group + group].reshape(64, 128)
        _, sums, delta_part = head(dense(feat_all[span, :].astype(jnp.bfloat16)), w_out, tails)
        delta_all[span, :] = delta_part
        grad_out = [old + new for old, new in zip(grad_out, sums)]
    square = (jnp.sum(grad_out[0] * grad_out[0]) + jnp.sum(grad_out[1] * grad_out[1])) / 4096.0
    for i in range(2):
        new_out[i : i + 1, :] = w_out[i : i + 1, :] - learn_rate * grad_out[i] * lax.rsqrt(
            square + rms_eps
        )

    total = grads[pl.ds(pl.multiple_of(me * per, 16), per), :].astype(jnp.float32)
    for hop in range(1, n):
        scatter[hop - 1].wait_recv()
        total = total + grads_in[hop].astype(jnp.float32)
    left = jnp.mean(total[:, :64] * total[:, :64], axis=1, keepdims=True) + rms_eps
    right = jnp.mean(total[:, 64:] * total[:, 64:], axis=1, keepdims=True) + rms_eps
    lane_all = lax.broadcasted_iota(jnp.int32, (per, 128), 1)
    update[me] = (total * jnp.where(lane_all < 64, lax.rsqrt(left), lax.rsqrt(right))).astype(
        jnp.bfloat16
    )
    gather = []
    for hop in range(1, n):
        peer = lax.rem(me + hop, n)
        gather.append(remote(update.at[me], update.at[me], sems, 6, hop, "stream", peer))
    for copy in gather:
        copy.start()

    if share % 128 == 0:
        own_feat = feat_all[:, pl.ds(pl.multiple_of(me * share, 128), share)]
    else:
        picks = lax.broadcasted_iota(jnp.int32, (2048, share), 0) - me * share
        hot = picks == lax.broadcasted_iota(jnp.int32, (2048, share), 1)
        own_feat = matmul(feat_all[...].astype(jnp.bfloat16), jnp.where(hot, 1.0, 0.0).astype(jnp.bfloat16))
    own_feat = own_feat.T.astype(jnp.bfloat16)
    for part in range(share // 64):
        grad = matmul(own_feat[part * 64 : part * 64 + 64], delta_all[...]) * scale_dense
        rate = learn_rate * lax.rsqrt(jnp.mean(grad * grad, axis=1, keepdims=True) + rms_eps)
        weight = w_vmem[pl.ds(pl.multiple_of(me * share + part * 64, 64), 64), :]
        new_hidden[part * 64 : part * 64 + 64, :] = weight.astype(jnp.float32) - grad * rate

    for copy in returns:
        copy.wait_recv()
    row_out = lax.broadcasted_iota(jnp.int32, (batch, 128), 0)
    for k in range(samples):
        line = jnp.zeros((batch, 128), jnp.float32)
        for hop in range(walls):
            away = (walls - hop) % walls
            spot = jnp.where(hops[k] == away, 2 * away + ranks[k], -1)
            line = line + jnp.where(row_out == spot, pred_in[hop], 0.0)
        stress[k : k + 1, :] = jnp.sum(line, axis=0, keepdims=True)
    for copy in gather:
        copy.wait_recv()
    step = update[...].reshape(n * per, 128).astype(jnp.float32) * learn_rate
    new_second[0:896, :] = k_second[0:896, :].astype(jnp.float32) - step[:896, :64]
    new_second[896:1728, :] = k_second[896:1728, :].astype(jnp.float32) - step[:832, 64:]
    new_first[...] = k_first[0:54, :].astype(jnp.float32) - step[832:886, 64:]
    for copy in copies + returns + scatter + gather + patches + targets + faces_y + faces_x:
        copy.wait_send()


def train(blocks, members, field, k_first, k_second, w_hidden, w_out):
    n, walls = lax.axis_size("stream"), lax.axis_size("wall")
    batch = CAP * walls
    slope, upper, lift = element_tables()
    tab_x = np.stack([slope.T, upper.T])[:, :, :, None] * np.ones((1, 1, 1, 128))
    tab_z = np.concatenate([axis_matrix(16, slope, lift).T, np.kron(np.eye(16), upper).T], axis=1)
    smem = pl.BlockSpec(memory_space=pltpu.SMEM)
    per = -(-896 // (n * 16)) * 16
    k_back = k_second.reshape(9, 3, 64, 64).transpose(0, 2, 1, 3).reshape(9, 64, 192)
    vmem = pl.BlockSpec(memory_space=pltpu.VMEM)
    return pl.pallas_call(
        functools.partial(network, n, walls, per),
        out_shape=(
            jax.ShapeDtypeStruct(field.shape, jnp.float32),
            jax.ShapeDtypeStruct((8, 128), jnp.float32),
            jax.ShapeDtypeStruct((54, 64), jnp.float32),
            jax.ShapeDtypeStruct((1728, 64), jnp.float32),
            jax.ShapeDtypeStruct((2048 // n, 2048), jnp.float32),
            jax.ShapeDtypeStruct((2, 2048), jnp.float32),
        ),
        in_specs=[smem] * 2 + [vmem] * 6 + [pl.BlockSpec(memory_space=pl.ANY), vmem],
        out_specs=(vmem,) * 6,
        scratch_shapes=[
            pltpu.VMEM((walls, 8, 256), jnp.float32),
            pltpu.VMEM((walls, 8, 128), jnp.float32),
            pltpu.VMEM((2048, 2048), jnp.bfloat16),
            pltpu.VMEM((64 * batch, 128), jnp.float32),
            pltpu.VMEM((128 * batch, 64), jnp.float32),
            pltpu.VMEM((6, 6, 8 * batch, 192), jnp.bfloat16),
            pltpu.VMEM((6, 6, 8 * batch, 192), jnp.bfloat16),
            pltpu.VMEM((6, 6, 8 * batch, 64), jnp.bfloat16),
            pltpu.VMEM((128 * batch, 64), jnp.float32),
            pltpu.VMEM((4, 8, batch, 64), jnp.float32),
            pltpu.VMEM((n, 2 * batch, 1024), jnp.bfloat16),
            pltpu.VMEM((n, batch, 128), jnp.float32),
            pltpu.VMEM((n * batch, 2048), jnp.float32),
            pltpu.VMEM((n * batch, 2048), jnp.bfloat16),
            pltpu.VMEM((n * per, 128), jnp.bfloat16),
            pltpu.VMEM((n, per, 128), jnp.bfloat16),
            pltpu.VMEM((n, per, 128), jnp.bfloat16),
            pltpu.VMEM((walls, batch, 128), jnp.float32),
            pltpu.VMEM((walls, 8, 256), jnp.float32),
            pltpu.VMEM((walls, 8, 128), jnp.float32),
            pltpu.VMEM((batch, 256), jnp.float32),
            pltpu.VMEM((batch, 128), jnp.float32),
            pltpu.VMEM((2, 3, 16, 128), jnp.float32),
            pltpu.VMEM((2, 3, 8, 128), jnp.float32),
            pltpu.VMEM((2, 3, 8, 128), jnp.float32),
            pltpu.SemaphoreType.DMA,
            pltpu.SemaphoreType.DMA((8, n)),
            pltpu.SemaphoreType.DMA((6, walls)),
            pltpu.SemaphoreType.DMA((4, 2)),
        ],
        compiler_params=pltpu.CompilerParams(
            vmem_limit_bytes=52 * 1024 * 1024, collective_id=0, has_side_effects=True
        ),
    )(
        blocks, members, field, jnp.asarray(tab_x, jnp.float32), jnp.asarray(tab_z, jnp.float32),
        jnp.pad(k_first, ((0, 10), (0, 0))), k_second.reshape(1728, 64), k_back, w_hidden,
        w_out.T.astype(jnp.float32),
    )


def body(velocity, sample_block, sample_member, k_first, k_second, w_hidden, w_out):
    samples = sample_block.shape[1]
    new_field, stress, new_first, new_second, new_w_hidden, new_out = train(
        sample_block, sample_member[:, :, 0], velocity, k_first[0], k_second[0], w_hidden[0], w_out[0]
    )
    return (
        new_field, stress[:samples, :2].T[:, None, :], new_first[None],
        new_second.reshape(k_second.shape), new_w_hidden[None], new_out.T[None],
    )


def solution(mesh):
    placed = (
        P(None, "wall", "stream", None),
        P("wall", "stream"),
        P("wall", "stream", None),
        P("wall", None, None),
        P("wall", None, None, None),
        P("wall", None, None),
        P("wall", None, None),
    )
    return jax.shard_map(
        body,
        mesh=mesh,
        in_specs=placed,
        out_specs=(
            P(None, "wall", "stream", None),
            P(None, "wall", "stream"),
            P("wall", None, None),
            P("wall", None, None, None),
            P("wall", "stream", None),
            P("wall", None, None),
        ),
        check_vma=False,
    )
```

```python
import functools
import math

import jax
import jax.numpy as jnp
import numpy as np
from jax import lax
from jax.experimental import pallas as pl
from jax.experimental.pallas import tpu as pltpu
from jax.sharding import PartitionSpec as P

P_SIZE = 8
CAP = 2


highest = lax.Precision.HIGHEST
time_step = 0.005
relax_rate = 20.0
viscosity = 0.3
learn_rate = 0.5
rms_eps = 1e-06
tap_offsets = [
    (first_off, second_off, third_off)
    for first_off in (-1, 0, 1)
    for second_off in (-1, 0, 1)
    for third_off in (-1, 0, 1)
]


def cheb_tables(points):
    order = points - 1
    node_index = np.arange(points)
    nodes = -np.cos(np.pi * node_index / order)
    end_weight = np.where((node_index == 0) | (node_index == order), 2.0, 1.0)
    parity = (-1.0) ** (node_index[:, None] + node_index[None, :])
    offdiag = 1.0 - np.eye(points)
    spread = nodes[:, None] - nodes[None, :] + np.eye(points)
    deriv = end_weight[:, None] / end_weight[None, :] * parity / spread * offdiag
    deriv = deriv - np.eye(points) * deriv.sum(axis=1)[:, None]
    highpass = parity / (order * end_weight[None, :])
    return (deriv, highpass, 0.5 * order * order)


def element_tables():
    slope, upper, lift = cheb_tables(P_SIZE)
    slope[0, 0] += lift
    slope[7, 7] -= lift
    return slope, upper, lift


def axis_matrix(count, slope, lift):
    whole = np.kron(np.eye(count), slope)
    for element in range(count):
        last_node = element * P_SIZE + P_SIZE - 1
        next_node = (element + 1) % count * P_SIZE
        whole[last_node, next_node] += lift
        whole[next_node, last_node] -= lift
    return whole


def sigmoid(value):
    return 1.0 / (1.0 + jnp.exp(-value))


def silu_slope(value):
    gate = sigmoid(value)
    return gate * (1.0 + value * (1.0 - gate))


def z_shifts(grid, sign):
    edge = jnp.zeros((16, 1, grid.shape[2], grid.shape[-1]), grid.dtype)
    before = jnp.concatenate([edge, grid[:, :-1]], axis=1)
    after = jnp.concatenate([grid[:, 1:], edge], axis=1)
    parts = [before, grid, after] if sign > 0 else [after, grid, before]
    return jnp.concatenate([part.reshape(-1, grid.shape[-1]) for part in parts], axis=-1)


def window(padded, first, second):
    return padded[1 + first : 5 + first, 1 + second : 5 + second].reshape(-1, padded.shape[-1])


def clear_border(padded):
    row = jnp.zeros((1, 6) + padded.shape[2:], padded.dtype)
    column = jnp.zeros((6, 1) + padded.shape[2:], padded.dtype)
    padded[0:1] = row
    padded[5:6] = row
    padded[:, 0:1] = column
    padded[:, 5:6] = column


def matmul(left, right, dims=((1,), (0,))):
    return lax.dot_general(left, right, (dims, ((), ())), preferred_element_type=jnp.float32)


def remote(source, target, semaphores, row, hop, axis, peer):
    return pltpu.make_async_remote_copy(
        src_ref=source, dst_ref=target,
        send_sem=semaphores.at[row, hop], recv_sem=semaphores.at[row + 1, hop],
        device_id={axis: peer}, device_id_type=pl.DeviceIdType.MESH,
    )


def head(third, w_out, tail):
    scale_dense = 1.0 / math.sqrt(2048.0)
    gate = sigmoid(third)
    hidden = (third * gate).astype(jnp.bfloat16).astype(jnp.float32)
    preds, errors, sums = [], [], []
    for i in range(2):
        pred = jnp.sum(hidden * w_out[i : i + 1, :], axis=1, keepdims=True) * scale_dense
        error = tail[:, 2:3] * (pred - tail[:, i : i + 1])
        sums.append(jnp.sum(hidden * error, axis=0, keepdims=True) * scale_dense)
        preds.append(pred)
        errors.append(error)
    outer = errors[0] * w_out[0:1, :] + errors[1] * w_out[1:2, :]
    delta = (outer * scale_dense * (gate * (1.0 + third * (1.0 - gate)))).astype(jnp.bfloat16)
    return preds, sums, delta


def network(
    n, walls, per, blocks, members, w_out, k_first, field_hbm, k_second_hbm, tab_x_hbm, tab_z_hbm, w_hbm,
    new_field, stress, new_first, new_second, new_hidden, new_out,
    patch_out, tail_out, w_vmem, cols, pre_one, hid_pad, del_pad, mid_pad, pre_two, pooled,
    feat_in, tail_in, feat_all, delta_all, grads, grads_in, update, pred_in,
    patch_in, tail_wall, rows_all, tails_all, face_y, face_x, edge_x,
    field, k_second, tab_x, tab_z, k_wide,
    load_sems, sems, wall_sems, face_sems,
):
    me, wall = lax.axis_index("stream"), lax.axis_index("wall")
    barrier = pltpu.get_barrier_semaphore()
    for hop in range(1, n):
        pl.semaphore_signal(
            barrier, inc=1, device_id={"stream": lax.rem(me + hop, n)},
            device_id_type=pl.DeviceIdType.MESH,
        )
    for hop in range(1, walls):
        pl.semaphore_signal(
            barrier, inc=1, device_id={"wall": lax.rem(wall + hop, walls)},
            device_id_type=pl.DeviceIdType.MESH,
        )
    batch = 2 * walls
    points = 128 * batch
    share = 2048 // n
    samples = blocks.shape[1]
    loads = [
        pltpu.make_async_copy(source, target, load_sems.at[i])
        for i, (source, target) in enumerate((
            (field_hbm, field), (k_second_hbm, k_second),
            (tab_x_hbm, tab_x), (tab_z_hbm, tab_z), (w_hbm, w_vmem),
        ))
    ]
    for load in loads:
        load.start()
    slope, upper, lift = element_tables()
    scale_one = 1.0 / math.sqrt(54.0)
    scale_two = 1.0 / math.sqrt(1728.0)
    scale_dense = 1.0 / math.sqrt(2048.0)
    clear_border(hid_pad)
    clear_border(del_pad)
    clear_border(mid_pad)
    lane = lax.broadcasted_iota(jnp.int32, (batch, 128), 1)
    at = (lane // 32, (lane // 8) % 4, lane % 8)
    cols[54 * batch : 64 * batch, :] = jnp.zeros((10 * batch, 128), jnp.float32)
    names = [members[0, k] for k in range(samples)]
    picks = [blocks[0, k] for k in range(samples)]
    ranks = []
    for k in range(samples):
        rank = jnp.int32(0)
        for j in range(k):
            rank = rank + jnp.where(names[j] == names[k], 1, 0)
        ranks.append(rank)
    hops = [lax.rem(name + walls - wall, walls) for name in names]

    def by_slot(shape):
        slot = lax.broadcasted_iota(jnp.int32, shape, 0) % batch
        found = jnp.full(shape, -1, jnp.int32)
        for k in range(samples):
            found = jnp.where(slot == hops[k] * 2 + ranks[k], picks[k], found)
        return found

    wide = (16 * batch, 128)
    found = by_slot(wide)
    point = lax.broadcasted_iota(jnp.int32, wide, 0) // batch
    lane_w = lax.broadcasted_iota(jnp.int32, wide, 1)
    row_at = ((found >> 6) * 4 + point // 4) * 16 + ((found >> 4) & 3) * 4 + point % 4
    row_hot = jnp.where((found >= 0) & (lane_w == row_at), 1.0, 0.0).astype(jnp.bfloat16)
    fold = jnp.where(
        lax.broadcasted_iota(jnp.int32, (128, 128), 0) % 8
        == lax.broadcasted_iota(jnp.int32, (128, 128), 1) % 8, 1.0, 0.0
    ).astype(jnp.bfloat16)
    loads[0].wait()
    for c in range(2):
        near = matmul(row_hot, field[2 * c].reshape(128, 128).astype(jnp.bfloat16))
        near = jnp.where(lane_w // 8 == (found & 15), near, 0.0).astype(jnp.bfloat16)
        folded = jnp.where(lane_w // 8 == point, matmul(near, fold), 0.0)
        folded = jnp.sum(folded.reshape(16, batch, 128), axis=0)
        rows_all[:, c * 128 : c * 128 + 128] = folded
    for hop in range(walls):
        patch_out[hop] = jnp.zeros((8, 256), jnp.float32)
        patch_out[hop, 0:2, :] = rows_all[2 * hop : 2 * hop + 2, :]
    edge_x[0] = field[:, :, 15, :]
    edge_x[1] = field[:, :, 0, :]
    pl.semaphore_wait(barrier, n + walls - 2)
    patches = []
    for hop in range(1, walls):
        peer = lax.rem(wall + hop, walls)
        patches.append(
            remote(patch_out.at[hop], patch_in.at[hop], wall_sems, 2, hop, "wall", peer)
        )
    above, below = lax.rem(wall + 1, walls), lax.rem(wall + walls - 1, walls)
    ahead, behind = lax.rem(me + 1, n), lax.rem(me + n - 1, n)
    faces_y = [
        remote(field.at[:, 7], face_y.at[0], face_sems, 0, 0, "wall", above),
        remote(field.at[:, 0], face_y.at[1], face_sems, 0, 1, "wall", below),
    ]
    faces_x = [
        remote(edge_x.at[0], face_x.at[0], face_sems, 2, 0, "stream", ahead),
        remote(edge_x.at[1], face_x.at[1], face_sems, 2, 1, "stream", behind),
    ]
    for copy in patches + faces_y + faces_x:
        copy.start()

    for copy in faces_y:
        copy.wait_recv()
    keep_low = jnp.where(wall > 0, lift, 0.0)
    keep_high = jnp.where(wall < walls - 1, lift, 0.0)
    found = by_slot((batch, 128))
    tail = jnp.where(lane == 2, jnp.where(found >= 0, 1.0, 0.0), 0.0)
    for i in range(2):
        halves = []
        for half in range(2):
            total = -keep_low * face_y[0, 2 * i] if half == 0 else keep_high * face_y[1, 2 * i]
            for j in range(8):
                weight = float(sum(slope[half * 4 : half * 4 + 4, j]))
                total = total + weight * field[2 * i, j]
            halves.append(total)
        mean = jnp.zeros((batch, 128), jnp.float32)
        for row in range(8):
            strip = halves[row // 4][row % 4 * 4 : row % 4 * 4 + 4, :]
            strip = jnp.sum(strip, axis=0, keepdims=True)
            mean = mean + jnp.where((found >> 4) == row, strip, 0.0)
        mean = jnp.where(lane // 8 == (found & 15), mean, 0.0)
        aim = jnp.sum(mean, axis=1, keepdims=True) * (viscosity / 128.0)
        tail = jnp.where((lane == i) & (found >= 0), aim.astype(jnp.bfloat16).astype(jnp.float32), tail)
    tails_all[...] = tail
    for hop in range(walls):
        tail_out[hop] = jnp.zeros((8, 128), jnp.float32)
        tail_out[hop, 0:2, :] = tails_all[2 * hop : 2 * hop + 2, :]
    targets = []
    for hop in range(1, walls):
        peer = lax.rem(wall + hop, walls)
        targets.append(
            remote(tail_out.at[hop], tail_wall.at[hop], wall_sems, 4, hop, "wall", peer)
        )
    for copy in targets:
        copy.start()

    for copy in patches:
        copy.wait_recv()
    for hop in range(1, walls):
        rows_all[2 * hop : 2 * hop + 2, :] = patch_in[hop, 0:2, :]
    channel = [rows_all[:, 0:128], rows_all[:, 128:256]]
    for tap, offset in enumerate(tap_offsets):
        inside = None
        for place, step, size in zip(at, offset, (4, 4, 8)):
            if step:
                good = (place + step >= 0) & (place + step < size)
                inside = good if inside is None else inside & good
        turn = (-(offset[0] * 32 + offset[1] * 8 + offset[2])) % 128
        for c in range(2):
            moved = channel[c] if turn == 0 else pltpu.roll(channel[c], turn, 1)
            if inside is not None:
                moved = jnp.where(inside, moved, 0.0)
            cols[(2 * tap + c) * batch : (2 * tap + c + 1) * batch, :] = moved
    columns = jnp.concatenate(
        [cols[pl.ds(slot, 64, stride=batch), :] for slot in range(batch)], axis=1
    ).astype(jnp.bfloat16)
    k_wide[...] = jnp.zeros((64, 64), jnp.float32)
    k_wide[0:54, :] = k_first[...].astype(jnp.float32)
    first = matmul(columns, k_wide[...].astype(jnp.bfloat16), ((0,), (0,))) * scale_one
    loads[1].wait()
    for slot in range(batch):
        pre_one[pl.ds(slot, 128, stride=batch), :] = first[slot * 128 : slot * 128 + 128]
    value = pre_one[...]
    hidden = (value * sigmoid(value)).astype(jnp.bfloat16).astype(jnp.float32)
    hidden3 = z_shifts(hidden.reshape(16, 8, batch, 64), 1)
    hidden_t = hidden3.T.astype(jnp.bfloat16)
    hid_pad[1:5, 1:5] = hidden3.astype(jnp.bfloat16).reshape(4, 4, 8 * batch, 192)
    total = jnp.zeros((points, 64), jnp.float32)
    for pair in range(9):
        total = total + matmul(window(hid_pad, pair // 3 - 1, pair % 3 - 1), k_second[pair * 192 : pair * 192 + 192, :])
    second = total * scale_two
    pre_two[...] = second
    act = (second * sigmoid(second)).reshape(2, 2, 2, 2, 8 * batch, 64)
    pool = (act[:, 0, :, 0] + act[:, 0, :, 1] + act[:, 1, :, 0] + act[:, 1, :, 1]) * 0.25
    pieces = pool.reshape(32, batch, 64)
    features = jnp.concatenate([pieces[i] for i in range(32)], axis=1)
    feat_in[0] = jnp.concatenate([features[:, :1024], features[:, 1024:]], axis=0).astype(
        jnp.bfloat16
    )
    for copy in targets:
        copy.wait_recv()
    for hop in range(1, walls):
        tails_all[2 * hop : 2 * hop + 2, :] = tail_wall[hop, 0:2, :]
    tail = tails_all[...]
    tail_in[0] = tail
    features = features.astype(jnp.bfloat16)
    copies = []
    for hop in range(1, n):
        peer = lax.rem(me + hop, n)
        copies.append(remote(feat_in.at[0], feat_in.at[hop], sems, 0, hop, "stream", peer))
        copies.append(remote(tail_in.at[0], tail_in.at[hop], sems, 2, hop, "stream", peer))
    for copy in copies:
        copy.start()
    loads[4].wait()

    def dense(values):
        return jnp.concatenate(
            [matmul(values, w_vmem[:, j * 512 : j * 512 + 512]) for j in range(4)], axis=1
        ) * scale_dense

    preds, _, delta_three = head(dense(features), w_out, tail)
    lane_out = lax.broadcasted_iota(jnp.int32, (batch, 128), 1)
    pred_in[0] = jnp.where(lane_out == 0, preds[0], jnp.where(lane_out == 1, preds[1], 0.0))
    returns = []
    for hop in range(1, walls):
        peer = lax.rem(wall + hop, walls)
        returns.append(remote(pred_in.at[0], pred_in.at[hop], wall_sems, 0, hop, "wall", peer))
    for copy in returns:
        copy.start()
    for j in range(8):
        back = matmul(delta_three, w_vmem[j * 256 : j * 256 + 256, :], ((1,), (1,)))
        for i in range(4):
            pooled[j // 2, (j % 2) * 4 + i] = back[:, i * 64 : i * 64 + 64]
    spread = (pooled[...] * (scale_dense * 0.25)).reshape(2, 1, 2, 1, 8 * batch, 64)
    spread = jnp.broadcast_to(spread, (2, 2, 2, 2, 8 * batch, 64)).reshape(points, 64)
    delta = (spread * silu_slope(pre_two[...])).astype(jnp.bfloat16).astype(jnp.float32)
    mid_pad[1:5, 1:5] = delta.astype(jnp.bfloat16).reshape(4, 4, 8 * batch, 64)
    delta3 = z_shifts(delta.reshape(16, 8, batch, 64), -1)
    del_pad[1:5, 1:5] = delta3.astype(jnp.bfloat16).reshape(4, 4, 8 * batch, 192)
    total = jnp.zeros((points, 64), jnp.float32)
    for pair in range(9):
        first_off, second_off = 1 - pair // 3, 1 - pair % 3
        grad_two = (matmul(hidden_t, window(mid_pad, first_off, second_off)) * scale_two).astype(
            jnp.bfloat16
        )
        start = pair * 192
        if start + 192 <= 896:
            grads[start : start + 192, 0:64] = grad_two
        elif start >= 896:
            grads[start - 896 : start - 704, 64:128] = grad_two
        else:
            grads[start:896, 0:64] = grad_two[: 896 - start]
            grads[0 : start - 704, 64:128] = grad_two[896 - start :]
        k_back = jnp.concatenate(
            [k_second[pair * 192 + c * 64 : pair * 192 + c * 64 + 64, :] for c in range(3)], axis=1
        )
        total = total + matmul(window(del_pad, first_off, second_off), k_back, ((1,), (1,)))
    pre_one[...] = total * scale_two * silu_slope(pre_one[...])
    delta_one = jnp.concatenate(
        [pre_one[pl.ds(slot, 128, stride=batch), :] for slot in range(batch)], axis=0
    ).astype(jnp.bfloat16)
    grads[832:896, 64:128] = (matmul(columns, delta_one) * scale_one).astype(jnp.bfloat16)
    if n * per > 896:
        grads[896 : n * per, :] = jnp.zeros((n * per - 896, 128), jnp.bfloat16)
    scatter = []
    for hop in range(1, n):
        peer = lax.rem(me + hop, n)
        chunk = grads.at[pl.ds(pl.multiple_of(peer * per, 16), per)]
        scatter.append(remote(chunk, grads_in.at[hop], sems, 4, hop, "stream", peer))
    for copy in scatter:
        copy.start()

    for copy in faces_x:
        copy.wait_recv()
    loads[2].wait()
    loads[3].wait()
    flow = field[...]
    split = flow.reshape(3, 8, 2, 8, 128)
    grad_x = jnp.zeros((3, 8, 2, 8, 128), jnp.float32)
    high = jnp.zeros((3, 8, 2, 8, 128), jnp.float32)
    for j in range(8):
        spread_j = split[:, :, :, j : j + 1, :]
        grad_x = grad_x + tab_x[0, j] * spread_j
        high = high + tab_x[1, j] * spread_j
    left_side = jnp.concatenate([face_x[0][:, :, None], split[:, :, 0:1, 7]], axis=2)[:, :, :, None]
    right_side = jnp.concatenate([split[:, :, 1:2, 0], face_x[1][:, :, None]], axis=2)[:, :, :, None]
    node = lax.broadcasted_iota(jnp.int32, (1, 1, 1, 8, 128), 3)
    grad_x = grad_x - jnp.where(node == 0, lift * left_side, 0.0)
    grad_x = grad_x + jnp.where(node == 7, lift * right_side, 0.0)
    grad_x = grad_x.reshape(3, 8, 16, 128)
    high = high.reshape(3, 8, 16, 128)
    along = lax.dot_general(
        flow.reshape(384, 128), tab_z[...], (((1,), (0,)), ((), ())),
        precision=highest, preferred_element_type=jnp.float32,
    )
    grad_z = along[:, :128].reshape(3, 8, 16, 128)
    high = high + along[:, 128:].reshape(3, 8, 16, 128)
    for i in range(8):
        grad_y = float(slope[i, 0]) * flow[:, 0]
        high_i = high[:, i] + float(upper[i, 0]) * flow[:, 0]
        for j in range(1, 8):
            grad_y = grad_y + float(slope[i, j]) * flow[:, j]
            high_i = high_i + float(upper[i, j]) * flow[:, j]
        if i == 0:
            grad_y = grad_y - keep_low * face_y[0]
        if i == 7:
            grad_y = grad_y + keep_high * face_y[1]
        advect = flow[0:1, i] * grad_x[:, i] + flow[1:2, i] * grad_y + flow[2:3, i] * grad_z[:, i]
        new_field[:, i] = flow[:, i] + time_step * (-advect - relax_rate * high_i)

    for copy in copies:
        copy.wait_recv()
    for hop in range(n):
        pair = feat_in[hop].astype(jnp.float32)
        feat_all[hop * batch : hop * batch + batch, 0:1024] = pair[:batch]
        feat_all[hop * batch : hop * batch + batch, 1024:2048] = pair[batch:]
    grad_out = [jnp.zeros((1, 2048), jnp.float32), jnp.zeros((1, 2048), jnp.float32)]
    group = 64 // batch
    for part in range(n // group):
        span = slice(part * 64, part * 64 + 64)
        tails = tail_in[part * group : part * group + group].reshape(64, 128)
        _, sums, delta_part = head(dense(feat_all[span, :].astype(jnp.bfloat16)), w_out, tails)
        delta_all[span, :] = delta_part
        grad_out = [old + new for old, new in zip(grad_out, sums)]
    square = (jnp.sum(grad_out[0] * grad_out[0]) + jnp.sum(grad_out[1] * grad_out[1])) / 4096.0
    for i in range(2):
        new_out[i : i + 1, :] = w_out[i : i + 1, :] - learn_rate * grad_out[i] * lax.rsqrt(
            square + rms_eps
        )

    total = grads[pl.ds(pl.multiple_of(me * per, 16), per), :].astype(jnp.float32)
    for hop in range(1, n):
        scatter[hop - 1].wait_recv()
        total = total + grads_in[hop].astype(jnp.float32)
    left = jnp.mean(total[:, :64] * total[:, :64], axis=1, keepdims=True) + rms_eps
    right = jnp.mean(total[:, 64:] * total[:, 64:], axis=1, keepdims=True) + rms_eps
    lane_all = lax.broadcasted_iota(jnp.int32, (per, 128), 1)
    update[me] = (total * jnp.where(lane_all < 64, lax.rsqrt(left), lax.rsqrt(right))).astype(
        jnp.bfloat16
    )
    gather = []
    for hop in range(1, n):
        peer = lax.rem(me + hop, n)
        gather.append(remote(update.at[me], update.at[me], sems, 6, hop, "stream", peer))
    for copy in gather:
        copy.start()

    if share % 128 == 0:
        own_feat = feat_all[:, pl.ds(pl.multiple_of(me * share, 128), share)]
    else:
        picks = lax.broadcasted_iota(jnp.int32, (2048, share), 0) - me * share
        hot = picks == lax.broadcasted_iota(jnp.int32, (2048, share), 1)
        own_feat = matmul(feat_all[...].astype(jnp.bfloat16), jnp.where(hot, 1.0, 0.0).astype(jnp.bfloat16))
    own_feat = own_feat.T.astype(jnp.bfloat16)
    for part in range(share // 64):
        grad = matmul(own_feat[part * 64 : part * 64 + 64], delta_all[...]) * scale_dense
        rate = learn_rate * lax.rsqrt(jnp.mean(grad * grad, axis=1, keepdims=True) + rms_eps)
        weight = w_vmem[pl.ds(pl.multiple_of(me * share + part * 64, 64), 64), :]
        new_hidden[part * 64 : part * 64 + 64, :] = weight.astype(jnp.float32) - grad * rate

    for copy in returns:
        copy.wait_recv()
    row_out = lax.broadcasted_iota(jnp.int32, (batch, 128), 0)
    for k in range(samples):
        line = jnp.zeros((batch, 128), jnp.float32)
        for hop in range(walls):
            away = (walls - hop) % walls
            spot = jnp.where(hops[k] == away, 2 * away + ranks[k], -1)
            line = line + jnp.where(row_out == spot, pred_in[hop], 0.0)
        stress[k : k + 1, :] = jnp.sum(line, axis=0, keepdims=True)
    for copy in gather:
        copy.wait_recv()
    step = update[...].reshape(n * per, 128).astype(jnp.float32) * learn_rate
    new_second[0:896, :] = k_second[0:896, :].astype(jnp.float32) - step[:896, :64]
    new_second[896:1728, :] = k_second[896:1728, :].astype(jnp.float32) - step[:832, 64:]
    new_first[...] = k_first[0:54, :].astype(jnp.float32) - step[832:886, 64:]
    for copy in copies + returns + scatter + gather + patches + targets + faces_y + faces_x:
        copy.wait_send()


def train(blocks, members, field, k_first, k_second, w_hidden, w_out):
    n, walls = lax.axis_size("stream"), lax.axis_size("wall")
    batch = CAP * walls
    slope, upper, lift = element_tables()
    tab_x = np.stack([slope.T, upper.T])[:, :, :, None] * np.ones((1, 1, 1, 128))
    tab_z = np.concatenate([axis_matrix(16, slope, lift).T, np.kron(np.eye(16), upper).T], axis=1)
    smem = pl.BlockSpec(memory_space=pltpu.SMEM)
    per = -(-896 // (n * 16)) * 16
    vmem = pl.BlockSpec(memory_space=pltpu.VMEM)
    return pl.pallas_call(
        functools.partial(network, n, walls, per),
        out_shape=(
            jax.ShapeDtypeStruct(field.shape, jnp.float32),
            jax.ShapeDtypeStruct((8, 128), jnp.float32),
            jax.ShapeDtypeStruct((54, 64), jnp.float32),
            jax.ShapeDtypeStruct((1728, 64), jnp.float32),
            jax.ShapeDtypeStruct((2048 // n, 2048), jnp.float32),
            jax.ShapeDtypeStruct((2, 2048), jnp.float32),
        ),
        in_specs=[smem] * 2 + [vmem] * 2 + [pl.BlockSpec(memory_space=pltpu.HBM)] * 5,
        out_specs=(vmem,) * 6,
        scratch_shapes=[
            pltpu.VMEM((walls, 8, 256), jnp.float32),
            pltpu.VMEM((walls, 8, 128), jnp.float32),
            pltpu.VMEM((2048, 2048), jnp.bfloat16),
            pltpu.VMEM((64 * batch, 128), jnp.float32),
            pltpu.VMEM((128 * batch, 64), jnp.float32),
            pltpu.VMEM((6, 6, 8 * batch, 192), jnp.bfloat16),
            pltpu.VMEM((6, 6, 8 * batch, 192), jnp.bfloat16),
            pltpu.VMEM((6, 6, 8 * batch, 64), jnp.bfloat16),
            pltpu.VMEM((128 * batch, 64), jnp.float32),
            pltpu.VMEM((4, 8, batch, 64), jnp.float32),
            pltpu.VMEM((n, 2 * batch, 1024), jnp.bfloat16),
            pltpu.VMEM((n, batch, 128), jnp.float32),
            pltpu.VMEM((n * batch, 2048), jnp.float32),
            pltpu.VMEM((n * batch, 2048), jnp.bfloat16),
            pltpu.VMEM((n * per, 128), jnp.bfloat16),
            pltpu.VMEM((n, per, 128), jnp.bfloat16),
            pltpu.VMEM((n, per, 128), jnp.bfloat16),
            pltpu.VMEM((walls, batch, 128), jnp.float32),
            pltpu.VMEM((walls, 8, 256), jnp.float32),
            pltpu.VMEM((walls, 8, 128), jnp.float32),
            pltpu.VMEM((batch, 256), jnp.float32),
            pltpu.VMEM((batch, 128), jnp.float32),
            pltpu.VMEM((2, 3, 16, 128), jnp.float32),
            pltpu.VMEM((2, 3, 8, 128), jnp.float32),
            pltpu.VMEM((2, 3, 8, 128), jnp.float32),
            pltpu.VMEM(field.shape, jnp.float32),
            pltpu.VMEM((1728, 64), jnp.bfloat16),
            pltpu.VMEM((2, 8, 8, 128), jnp.float32),
            pltpu.VMEM((128, 256), jnp.float32),
            pltpu.VMEM((64, 64), jnp.float32),
            pltpu.SemaphoreType.DMA((5,)),
            pltpu.SemaphoreType.DMA((8, n)),
            pltpu.SemaphoreType.DMA((6, walls)),
            pltpu.SemaphoreType.DMA((4, 2)),
        ],
        compiler_params=pltpu.CompilerParams(
            vmem_limit_bytes=60 * 1024 * 1024, collective_id=0, has_side_effects=True
        ),
    )(
        blocks, members, w_out.T.astype(jnp.float32), k_first, field, k_second.reshape(1728, 64),
        jnp.asarray(tab_x, jnp.float32), jnp.asarray(tab_z, jnp.float32), w_hidden,
    )


def body(velocity, sample_block, sample_member, k_first, k_second, w_hidden, w_out):
    samples = sample_block.shape[1]
    new_field, stress, new_first, new_second, new_w_hidden, new_out = train(
        sample_block, sample_member[:, :, 0], velocity, k_first[0], k_second[0], w_hidden[0], w_out[0]
    )
    return (
        new_field, stress[:samples, :2].T[:, None, :], new_first[None],
        new_second.reshape(k_second.shape), new_w_hidden[None], new_out.T[None],
    )


def solution(mesh):
    placed = (
        P(None, "wall", "stream", None),
        P("wall", "stream"),
        P("wall", "stream", None),
        P("wall", None, None),
        P("wall", None, None, None),
        P("wall", None, None),
        P("wall", None, None),
    )
    return jax.shard_map(
        body,
        mesh=mesh,
        in_specs=placed,
        out_specs=(
            P(None, "wall", "stream", None),
            P(None, "wall", "stream"),
            P("wall", None, None),
            P("wall", None, None, None),
            P("wall", "stream", None),
            P("wall", None, None),
        ),
        check_vma=False,
    )
```
